32 devices in a mesh: group: 2 (over y), col: 4 (over z), sec: 2 (over x), lev: 2 (over core).
Axes of the slice: x: 2, y: 2, z: 4, core: 2. Of those that a mesh axis runs over, the one named last changes fastest.
Arguments:
- thermal_departure: bfloat16 [60, 512, 512], P('lev', ('group', 'col'), 'sec'), parts along dimension 1, may hold values from -6 to 6
- seed_sensitivity: float32 [60, 512, 512], P('lev', ('group', 'col'), 'sec'), parts along dimension 1, may hold values from -6 to 6
- zonal_flow_ratio: float32 [60, 512, 512], P('lev', ('group', 'col'), 'sec'), parts along dimension 1, may hold values from 0.3 to 0.6
- meridional_flow_ratio: float32 [60, 512, 512], P('lev', ('group', 'col'), 'sec'), parts along dimension 1, may hold values from 0.05 to 0.2
- updraft_flow_ratio: float32 [60, 512, 512], P('lev', ('group', 'col'), 'sec'), parts along dimension 1, may hold values from 0.05 to 0.2
- entry_layer_matrix: float32 [60, 256], replicated, may hold values from -0.75 to 0.75
- final_layer_matrix: float32 [256, 60], replicated, may hold values from -0.375 to 0.375
- mean_estimate_entry_matrix: float32 [60, 256], P(None, ('col', 'sec', 'lev')), may hold values from -6 to 6
- squared_estimate_entry_matrix: float32 [60, 256], P(None, ('col', 'sec', 'lev')), may hold values from 0.1 to 2
- mean_estimate_final_matrix: float32 [256, 60], P(('col', 'sec', 'lev')), may hold values from -6 to 6
- squared_estimate_final_matrix: float32 [256, 60], P(('col', 'sec', 'lev')), may hold values from 0.1 to 2
Outputs:
- input_cotangent: float32 [60, 512, 512], P('lev', ('group', 'col'), 'sec'), parts along dimension 1
- new_w_in: float32 [120, 256], P('group'), parts along dimension 0
- new_w_out: float32 [512, 60], P('group'), parts along dimension 0
- new_first_in: float32 [120, 256], P('group', ('col', 'sec', 'lev')), parts along dimension 0
- new_second_in: float32 [120, 256], P('group', ('col', 'sec', 'lev')), parts along dimension 0
- new_first_out: float32 [512, 60], P(('group', 'col', 'sec', 'lev')), parts along dimension 0
- new_second_out: float32 [512, 60], P(('group', 'col', 'sec', 'lev')), parts along dimension 0
The draws below stay inside these ranges and needn't reach their ends.
There are 2 independent parts, one for each index of `group`. The reference program is written for one: setup_inputs(seed, part) draws one part's arguments, and reference() takes and returns one part's arrays. A program takes and returns all parts, laid end to end along the dimension named above; an argument that names none is the same for every part. Nothing has to cross between parts.
All inputs are finite; a program needn't handle non-finite values.
Results may differ from the reference program's by a relative error of at most 0.0003.
The reference program's roundings to bfloat16 on the way (of `costate_bf`, `act_bf`, `d_pre` and `d_input`) count: a program that leaves them out, or rounds other values in their place, can miss the bound.
Values may be sent and summed in bfloat16 or wider, within the bound.
A program may use at most 128 MiB of HBM per device.

```python
import math
import jax
import jax.numpy as jnp
from jax import lax

HEIGHT_LAYERS = 60
HIDDEN_SIZE = 256
LOCAL_ZONAL_SPAN = 64
STEPS = 4
ZONAL_CELLS = 256
MERIDIONAL_CELLS = 512
COLUMNS = 131072


def steps_of(key, extent, split, smallest, high):
    gain, own = 1.0, jax.random.fold_in(key, 6)
    for axis_at, parts in split:
        steps = jnp.exp(jax.random.uniform(jax.random.fold_in(own, axis_at), (parts,), jnp.float32, smallest / len(split), high / len(split)))
        gain = gain * jnp.repeat(steps, extent[axis_at] // parts).reshape([-1 if axis == axis_at else 1 for axis in range(len(extent))])
    return gain


def centred(rng, extent, width, bound, cuts=(), kind=jnp.bfloat16):
    gain = steps_of(rng, extent, cuts, -0.22, 0.18) if cuts else 1.0
    entries = jax.random.normal(rng, extent, jnp.float32) * width * gain
    return jnp.minimum(jnp.maximum(entries, -bound), bound).astype(kind)


def setup_inputs(seed: int = 0, part: int = 0) -> dict:
    splits = jax.random.split(jax.random.key(seed), 12)
    part_keys = jax.random.split(jax.random.fold_in(splits[11], part), 12)
    thermal_departure = centred(part_keys[0], (HEIGHT_LAYERS, ZONAL_CELLS, MERIDIONAL_CELLS), 1.0, 6.0, ((0, 2), (1, 4), (2, 2)))
    seed_sensitivity = centred(part_keys[1], (HEIGHT_LAYERS, ZONAL_CELLS, MERIDIONAL_CELLS), 1.0, 6.0, ((0, 2), (1, 4), (2, 2)), jnp.float32)
    zonal_flow_ratio = jnp.clip(0.3 + 0.3 * jax.random.uniform(part_keys[2], (HEIGHT_LAYERS, ZONAL_CELLS, MERIDIONAL_CELLS), jnp.float32) ** steps_of(part_keys[2], (HEIGHT_LAYERS, ZONAL_CELLS, MERIDIONAL_CELLS), ((0, 2), (1, 4), (2, 2)), -0.2, 0.2), 0.3, 0.6)
    meridional_flow_ratio = jnp.clip(0.05 + 0.15 * jax.random.uniform(part_keys[3], (HEIGHT_LAYERS, ZONAL_CELLS, MERIDIONAL_CELLS), jnp.float32) ** steps_of(part_keys[3], (HEIGHT_LAYERS, ZONAL_CELLS, MERIDIONAL_CELLS), ((0, 2), (1, 4), (2, 2)), -0.2, 0.2), 0.05, 0.2)
    updraft_flow_ratio = jnp.clip(0.05 + 0.15 * jax.random.uniform(part_keys[4], (HEIGHT_LAYERS, ZONAL_CELLS, MERIDIONAL_CELLS), jnp.float32) ** steps_of(part_keys[4], (HEIGHT_LAYERS, ZONAL_CELLS, MERIDIONAL_CELLS), ((0, 2), (1, 4), (2, 2)), -0.2, 0.2), 0.05, 0.2)
    entry_layer_matrix = centred(splits[5], (HEIGHT_LAYERS, HIDDEN_SIZE), HEIGHT_LAYERS ** -0.5, 0.75, (), jnp.float32)
    final_layer_matrix = centred(splits[6], (HIDDEN_SIZE, HEIGHT_LAYERS), HIDDEN_SIZE ** -0.5, 0.375, (), jnp.float32)
    mean_estimate_entry_matrix = centred(splits[7], (HEIGHT_LAYERS, HIDDEN_SIZE), 1.0, 6.0, ((1, 16),), jnp.float32)
    squared_estimate_entry_matrix = jnp.clip(jnp.exp(math.log(2.0) - 2.9957323 * jax.random.uniform(splits[8], (HEIGHT_LAYERS, HIDDEN_SIZE), jnp.float32) ** steps_of(splits[8], (HEIGHT_LAYERS, HIDDEN_SIZE), ((1, 16),), -0.2, 0.2)), 0.1, 2.0)
    mean_estimate_final_matrix = centred(splits[9], (HIDDEN_SIZE, HEIGHT_LAYERS), 1.0, 6.0, ((0, 16),), jnp.float32)
    squared_estimate_final_matrix = jnp.clip(jnp.exp(math.log(2.0) - 2.9957323 * jax.random.uniform(splits[10], (HIDDEN_SIZE, HEIGHT_LAYERS), jnp.float32) ** steps_of(splits[10], (HIDDEN_SIZE, HEIGHT_LAYERS), ((0, 16),), -0.2, 0.2)), 0.1, 2.0)
    return {"thermal_departure": thermal_departure, "seed_sensitivity": seed_sensitivity, "zonal_flow_ratio": zonal_flow_ratio, "meridional_flow_ratio": meridional_flow_ratio, "updraft_flow_ratio": updraft_flow_ratio, "entry_layer_matrix": entry_layer_matrix, "final_layer_matrix": final_layer_matrix, "mean_estimate_entry_matrix": mean_estimate_entry_matrix, "squared_estimate_entry_matrix": squared_estimate_entry_matrix, "mean_estimate_final_matrix": mean_estimate_final_matrix, "squared_estimate_final_matrix": squared_estimate_final_matrix}


bias_first = 1.0 - 0.9 ** 10
bias_second = 1.0 - 0.999 ** 10

def adjoint_step(costate, zonal_flow_ratio, meridional_flow_ratio, updraft_flow_ratio):
    next_x = jnp.roll(costate, -1, axis=1)
    next_y = jnp.concatenate([costate[:, :, 1:], jnp.zeros_like(costate[:, :, :1])], axis=2)
    next_z = jnp.concatenate([costate[1:], jnp.zeros_like(costate[:1])], axis=0)
    return costate + zonal_flow_ratio * (next_x - costate) + meridional_flow_ratio * (next_y - costate) + updraft_flow_ratio * (next_z - costate)

def adam_update(weight, grad, first, second):
    new_first = 0.9 * first + 0.1 * grad
    new_second = 0.999 * second + 0.001 * grad * grad
    step_size = new_first / bias_first / (jnp.sqrt(new_second / bias_second) + 1e-08)
    return (weight - 0.01 * step_size, new_first, new_second)

def reference(thermal_departure, seed_sensitivity, zonal_flow_ratio, meridional_flow_ratio, updraft_flow_ratio, entry_layer_matrix, final_layer_matrix, mean_estimate_entry_matrix, squared_estimate_entry_matrix, mean_estimate_final_matrix, squared_estimate_final_matrix):
    costate = seed_sensitivity
    for step in range(STEPS):
        costate = adjoint_step(costate, zonal_flow_ratio, meridional_flow_ratio, updraft_flow_ratio)
    costate_bf = costate.astype(jnp.bfloat16)
    w_in_bf = entry_layer_matrix.astype(jnp.bfloat16)
    w_out_bf = final_layer_matrix.astype(jnp.bfloat16)
    blocks = ZONAL_CELLS // LOCAL_ZONAL_SPAN

    def one_block(carry, index):
        leading_position = (index * LOCAL_ZONAL_SPAN).astype(jnp.int32)
        stacked_height_slice = lax.dynamic_slice_in_dim(thermal_departure, leading_position, LOCAL_ZONAL_SPAN, 1).reshape(HEIGHT_LAYERS, LOCAL_ZONAL_SPAN * MERIDIONAL_CELLS)
        back = lax.dynamic_slice_in_dim(costate_bf, leading_position, LOCAL_ZONAL_SPAN, 1).reshape(HEIGHT_LAYERS, LOCAL_ZONAL_SPAN * MERIDIONAL_CELLS)
        pre = lax.dot_general(w_in_bf, stacked_height_slice, (((0,), (0,)), ((), ())), preferred_element_type=jnp.float32)
        act = jnp.tanh(pre)
        act_bf = act.astype(jnp.bfloat16)
        part_out = lax.dot_general(act_bf, back, (((1,), (1,)), ((), ())), preferred_element_type=jnp.float32)
        d_act = jnp.dot(w_out_bf, back, preferred_element_type=jnp.float32)
        d_pre = (d_act * (1.0 - act * act)).astype(jnp.bfloat16)
        part_in = lax.dot_general(stacked_height_slice, d_pre, (((1,), (1,)), ((), ())), preferred_element_type=jnp.float32)
        d_input = jnp.dot(w_in_bf, d_pre, preferred_element_type=jnp.float32).astype(jnp.bfloat16)
        return ((carry[0] + part_in, carry[1] + part_out), d_input.reshape(HEIGHT_LAYERS, LOCAL_ZONAL_SPAN, MERIDIONAL_CELLS))
    init = (jnp.zeros((HEIGHT_LAYERS, HIDDEN_SIZE), jnp.float32), jnp.zeros((HIDDEN_SIZE, HEIGHT_LAYERS), jnp.float32))
    sums, pieces = lax.scan(one_block, init, jnp.arange(blocks, dtype=jnp.int32))
    d_input = jnp.transpose(pieces, (1, 0, 2, 3)).reshape(HEIGHT_LAYERS, ZONAL_CELLS, MERIDIONAL_CELLS)
    input_cotangent = costate + d_input.astype(jnp.float32)
    factor = 1.0 / math.sqrt(COLUMNS)
    grad_in = sums[0] * factor
    grad_out = sums[1] * factor
    new_w_in, new_first_in, new_second_in = adam_update(entry_layer_matrix, grad_in, mean_estimate_entry_matrix, squared_estimate_entry_matrix)
    new_w_out, new_first_out, new_second_out = adam_update(final_layer_matrix, grad_out, mean_estimate_final_matrix, squared_estimate_final_matrix)
    return (input_cotangent, new_w_in, new_w_out, new_first_in, new_second_in, new_first_out, new_second_out)
```

```python
import functools
import math

import jax
import jax.numpy as jnp
from jax import lax
from jax.experimental import pallas as pl
from jax.experimental.pallas import tpu as pltpu
from jax.sharding import PartitionSpec as P

STEPS = 4


bias_first = 1.0 - 0.9**10
bias_second = 1.0 - 0.999**10


def passed_along(value, axis, steps):
    count = lax.axis_size(axis)
    pairs = [(source, (source + steps) % count) for source in range(count)]
    return lax.ppermute(value, axis, pairs)


def from_behind(value, axis, steps):
    count = lax.axis_size(axis)
    first, last = (max(0, -steps), min(count, count - steps))
    return lax.ppermute(value, axis, [(source, source + steps) for source in range(first, last)])


def adam_update(weight, grad, first, second):
    new_first = 0.9 * first + 0.1 * grad
    new_second = 0.999 * second + 0.001 * grad * grad
    step_size = new_first / bias_first / (jnp.sqrt(new_second / bias_second) + 1e-08)
    return (weight - 0.01 * step_size, new_first, new_second)


def adjoint_step(costate, zonal_flow_ratio, meridional_flow_ratio, updraft_flow_ratio):
    edge_x = passed_along(costate[:, 0:1, :], "col", -1)
    edge_y = from_behind(costate[:, :, 0:1], "sec", -1)
    edge_z = from_behind(costate[0:1], "lev", -1)
    next_x = jnp.concatenate([costate[:, 1:, :], edge_x], axis=1)
    next_y = jnp.concatenate([costate[:, :, 1:], edge_y], axis=2)
    next_z = jnp.concatenate([costate[1:], edge_z], axis=0)
    return (
        costate
        + zonal_flow_ratio * (next_x - costate)
        + meridional_flow_ratio * (next_y - costate)
        + updraft_flow_ratio * (next_z - costate)
    )


def transport(seed_sensitivity, zonal_flow_ratio, meridional_flow_ratio, updraft_flow_ratio):
    costate = seed_sensitivity
    for step in range(STEPS):
        costate = adjoint_step(costate, zonal_flow_ratio, meridional_flow_ratio, updraft_flow_ratio)
    return costate


MESH = pl.DeviceIdType.MESH
REDUCED = ("col", "sec", "lev")


def slot_size(levels):
    return -(-levels // 8) * 8


def slots(value, parts):
    levels = value.shape[1] // parts
    value = value.reshape(value.shape[0], parts, levels)
    value = jnp.pad(value, ((0, 0), (0, 0), (0, slot_size(levels) - levels)))
    return value.reshape(value.shape[0], -1)


def unslots(value, parts, levels_all):
    slot = value.shape[1] // parts
    value = value.reshape(value.shape[0], parts, slot)[:, :, : levels_all // parts]
    return value.reshape(value.shape[0], levels_all)


def peer_at(position, sizes):
    _, secs, levs = sizes
    return {
        "col": lax.div(position, secs * levs),
        "sec": lax.rem(lax.div(position, levs), secs),
        "lev": lax.rem(position, levs),
    }


def own_position(sizes):
    _, secs, levs = sizes
    return (lax.axis_index("col") * secs + lax.axis_index("sec")) * levs + lax.axis_index("lev")


def reduce_kernel(
    sizes, factor, grad_ref, weight_ref, first_ref, second_ref,
    new_weight_ref, new_first_ref, new_second_ref,
    landed, piece, send_sems, recv_sems, out_sems, in_sems,
):
    count = sizes[0] * sizes[1] * sizes[2]
    me = own_position(sizes)
    barrier = pltpu.get_barrier_semaphore()

    def greet(hop, carry):
        peer = lax.rem(me + hop, count)
        pl.semaphore_signal(barrier, inc=1, device_id=peer_at(peer, sizes), device_id_type=MESH)
        return carry

    lax.fori_loop(1, count, greet, 0)
    pl.semaphore_wait(barrier, count - 1)

    def share(hop):
        peer = lax.rem(me + hop, count)
        return pltpu.make_async_remote_copy(
            src_ref=grad_ref.at[peer], dst_ref=landed.at[hop],
            send_sem=send_sems.at[hop], recv_sem=recv_sems.at[hop],
            device_id=peer_at(peer, sizes), device_id_type=MESH,
        )

    def spread(hop):
        peer = lax.rem(me + hop, count)
        return pltpu.make_async_remote_copy(
            src_ref=piece, dst_ref=new_weight_ref.at[me],
            send_sem=out_sems.at[hop], recv_sem=in_sems.at[hop],
            device_id=peer_at(peer, sizes), device_id_type=MESH,
        )

    def start(make):
        def body(hop, carry):
            make(hop).start()
            return carry
        lax.fori_loop(1, count, body, 0)

    start(share)

    def add(hop, total):
        share(hop).wait_recv()
        return total + landed[hop]

    total = lax.fori_loop(1, count, add, grad_ref[me])
    piece[...], new_first_ref[...], new_second_ref[...] = adam_update(
        weight_ref[me], total * factor, first_ref[...], second_ref[...]
    )
    start(spread)
    new_weight_ref[me] = piece[...]

    def arrive(hop, carry):
        spread(hop).wait_recv()
        return carry

    def leave(hop, carry):
        share(hop).wait_send()
        spread(hop).wait_send()
        return carry

    lax.fori_loop(1, count, arrive, 0)
    lax.fori_loop(1, count, leave, 0)


def reduce_update(sizes, factor, grad, weight, first, second):
    count = sizes[0] * sizes[1] * sizes[2]
    rows, lanes = first.shape
    vmem = pl.BlockSpec(memory_space=pltpu.VMEM)
    dma = pltpu.SemaphoreType.DMA((count,))
    new_weight, new_first, new_second = pl.pallas_call(
        functools.partial(reduce_kernel, sizes, factor),
        out_shape=[
            jax.ShapeDtypeStruct((count, rows, lanes), jnp.float32),
            jax.ShapeDtypeStruct((rows, lanes), jnp.float32),
            jax.ShapeDtypeStruct((rows, lanes), jnp.float32),
        ],
        in_specs=[vmem] * 4,
        out_specs=[vmem] * 3,
        scratch_shapes=[
            pltpu.VMEM((count, rows, lanes), jnp.float32),
            pltpu.VMEM((rows, lanes), jnp.float32),
            dma, dma, dma, dma,
        ],
        compiler_params=pltpu.CompilerParams(collective_id=1, has_side_effects=True),
        name="reduce_update",
    )(grad.reshape(count, rows, lanes), weight.reshape(count, rows, lanes), first, second)
    return new_weight.reshape(count * rows, lanes), new_first, new_second


def shards(
    thermal_departure,
    seed_sensitivity,
    zonal_flow_ratio,
    meridional_flow_ratio,
    updraft_flow_ratio,
    entry_layer_matrix,
    final_layer_matrix,
    mean_estimate_entry_matrix,
    squared_estimate_entry_matrix,
    mean_estimate_final_matrix,
    squared_estimate_final_matrix,
):
    levels_all = entry_layer_matrix.shape[0]
    w_in_bf = entry_layer_matrix.astype(jnp.bfloat16)
    w_out_bf = final_layer_matrix.astype(jnp.bfloat16)
    total_cols = (
        seed_sensitivity.shape[1]
        * seed_sensitivity.shape[2]
        * lax.axis_size("col")
        * lax.axis_size("sec")
    )
    factor = 1.0 / math.sqrt(total_cols)
    costate = transport(
        seed_sensitivity, zonal_flow_ratio, meridional_flow_ratio, updraft_flow_ratio
    )
    costate_bf = costate.astype(jnp.bfloat16)
    profiles, back_cols = (
        lax.all_to_all(thermal_departure, "lev", split_axis=1, concat_axis=0, tiled=True),
        lax.all_to_all(costate_bf, "lev", split_axis=1, concat_axis=0, tiled=True),
    )
    flat = profiles.reshape(levels_all, -1)
    pre = lax.dot_general(
        w_in_bf, flat, (((0,), (0,)), ((), ())), preferred_element_type=jnp.float32
    )
    act = jnp.tanh(pre)
    col_shape = back_cols.shape
    back = back_cols.reshape(levels_all, -1)
    act_bf = act.astype(jnp.bfloat16)
    part_out = lax.dot_general(
        act_bf, back, (((1,), (1,)), ((), ())), preferred_element_type=jnp.float32
    )
    d_act = jnp.dot(w_out_bf, back, preferred_element_type=jnp.float32)
    d_pre = (d_act * (1.0 - act * act)).astype(jnp.bfloat16)
    part_in = lax.dot_general(
        flat, d_pre, (((1,), (1,)), ((), ())), preferred_element_type=jnp.float32
    )
    d_input = jnp.dot(w_in_bf, d_pre, preferred_element_type=jnp.float32).astype(jnp.bfloat16)
    d_levels = lax.all_to_all(
        d_input.reshape(col_shape), "lev", split_axis=0, concat_axis=1, tiled=True
    )
    input_cotangent = costate + d_levels.astype(jnp.float32)
    sizes = tuple(lax.axis_size(axis) for axis in REDUCED)
    levs = sizes[2]

    def packed(of_out, of_in):
        return jnp.concatenate([slots(of_out, levs), slots(of_in.T, levs)], axis=1)

    def unpacked(value):
        half = value.shape[1] // 2
        return (
            unslots(value[:, half:], levs, levels_all).T,
            unslots(value[:, :half], levs, levels_all),
        )

    new_weight, new_first, new_second = reduce_update(
        sizes, factor, packed(part_out, part_in), packed(final_layer_matrix, entry_layer_matrix),
        packed(mean_estimate_final_matrix, mean_estimate_entry_matrix),
        packed(squared_estimate_final_matrix, squared_estimate_entry_matrix),
    )
    new_w_in, new_w_out = unpacked(new_weight)
    new_first_in, new_first_out = unpacked(new_first)
    new_second_in, new_second_out = unpacked(new_second)
    return (
        input_cotangent,
        new_w_in,
        new_w_out,
        new_first_in,
        new_second_in,
        new_first_out,
        new_second_out,
    )


def solution(mesh):
    in_specs = (
        P("lev", ("group", "col"), "sec"),
        P("lev", ("group", "col"), "sec"),
        P("lev", ("group", "col"), "sec"),
        P("lev", ("group", "col"), "sec"),
        P("lev", ("group", "col"), "sec"),
        P(),
        P(),
        P(None, ("col", "sec", "lev")),
        P(None, ("col", "sec", "lev")),
        P(("col", "sec", "lev"), None),
        P(("col", "sec", "lev"), None),
    )
    out_specs = (
        P("lev", ("group", "col"), "sec"),
        P("group", None),
        P("group", None),
        P("group", ("col", "sec", "lev")),
        P("group", ("col", "sec", "lev")),
        P(("group", "col", "sec", "lev"), None),
        P(("group", "col", "sec", "lev"), None),
    )
    return jax.shard_map(shards, mesh=mesh, in_specs=in_specs, out_specs=out_specs, check_vma=False)
```

```python
import functools
import math

import jax
import jax.numpy as jnp
from jax import lax
from jax.experimental import pallas as pl
from jax.experimental.pallas import tpu as pltpu
from jax.sharding import PartitionSpec as P

STEPS = 4


bias_first = 1.0 - 0.9**10
bias_second = 1.0 - 0.999**10


def adam_update(weight, grad, first, second):
    new_first = 0.9 * first + 0.1 * grad
    new_second = 0.999 * second + 0.001 * grad * grad
    step_size = new_first / bias_first / (jnp.sqrt(new_second / bias_second) + 1e-08)
    return (weight - 0.01 * step_size, new_first, new_second)


MESH = pl.DeviceIdType.MESH
REDUCED = ("col", "sec", "lev")


def slot_size(levels):
    return -(-levels // 8) * 8


def slots(value, parts):
    levels = value.shape[1] // parts
    value = value.reshape(value.shape[0], parts, levels)
    value = jnp.pad(value, ((0, 0), (0, 0), (0, slot_size(levels) - levels)))
    return value.reshape(value.shape[0], -1)


def unslots(value, parts, levels_all):
    slot = value.shape[1] // parts
    value = value.reshape(value.shape[0], parts, slot)[:, :, : levels_all // parts]
    return value.reshape(value.shape[0], levels_all)


def peer_at(position, sizes):
    _, secs, levs = sizes
    return {
        "col": lax.div(position, secs * levs),
        "sec": lax.rem(lax.div(position, levs), secs),
        "lev": lax.rem(position, levs),
    }


def own_position(sizes):
    _, secs, levs = sizes
    return (lax.axis_index("col") * secs + lax.axis_index("sec")) * levs + lax.axis_index("lev")


def reduce_kernel(
    sizes, factor, grad_ref, weight_ref, first_ref, second_ref,
    new_weight_ref, new_first_ref, new_second_ref,
    landed, piece, send_sems, recv_sems, out_sems, in_sems,
):
    count = sizes[0] * sizes[1] * sizes[2]
    me = own_position(sizes)
    barrier = pltpu.get_barrier_semaphore()

    def greet(hop, carry):
        peer = lax.rem(me + hop, count)
        pl.semaphore_signal(barrier, inc=1, device_id=peer_at(peer, sizes), device_id_type=MESH)
        return carry

    lax.fori_loop(1, count, greet, 0)
    pl.semaphore_wait(barrier, count - 1)

    def share(hop):
        peer = lax.rem(me + hop, count)
        return pltpu.make_async_remote_copy(
            src_ref=grad_ref.at[peer], dst_ref=landed.at[hop],
            send_sem=send_sems.at[hop], recv_sem=recv_sems.at[hop],
            device_id=peer_at(peer, sizes), device_id_type=MESH,
        )

    def spread(hop):
        peer = lax.rem(me + hop, count)
        return pltpu.make_async_remote_copy(
            src_ref=piece, dst_ref=new_weight_ref.at[me],
            send_sem=out_sems.at[hop], recv_sem=in_sems.at[hop],
            device_id=peer_at(peer, sizes), device_id_type=MESH,
        )

    def start(make):
        def body(hop, carry):
            make(hop).start()
            return carry
        lax.fori_loop(1, count, body, 0)

    start(share)

    def add(hop, total):
        share(hop).wait_recv()
        return total + landed[hop]

    total = lax.fori_loop(1, count, add, grad_ref[me])
    piece[...], new_first_ref[...], new_second_ref[...] = adam_update(
        weight_ref[me], total * factor, first_ref[...], second_ref[...]
    )
    start(spread)
    new_weight_ref[me] = piece[...]

    def arrive(hop, carry):
        spread(hop).wait_recv()
        return carry

    def leave(hop, carry):
        share(hop).wait_send()
        spread(hop).wait_send()
        return carry

    lax.fori_loop(1, count, arrive, 0)
    lax.fori_loop(1, count, leave, 0)


def reduce_update(sizes, factor, grad, weight, first, second):
    count = sizes[0] * sizes[1] * sizes[2]
    rows, lanes = first.shape
    vmem = pl.BlockSpec(memory_space=pltpu.VMEM)
    dma = pltpu.SemaphoreType.DMA((count,))
    new_weight, new_first, new_second = pl.pallas_call(
        functools.partial(reduce_kernel, sizes, factor),
        out_shape=[
            jax.ShapeDtypeStruct((count, rows, lanes), jnp.float32),
            jax.ShapeDtypeStruct((rows, lanes), jnp.float32),
            jax.ShapeDtypeStruct((rows, lanes), jnp.float32),
        ],
        in_specs=[vmem] * 4,
        out_specs=[vmem] * 3,
        scratch_shapes=[
            pltpu.VMEM((count, rows, lanes), jnp.float32),
            pltpu.VMEM((rows, lanes), jnp.float32),
            dma, dma, dma, dma,
        ],
        compiler_params=pltpu.CompilerParams(collective_id=1, has_side_effects=True),
        name="reduce_update",
    )(grad.reshape(count, rows, lanes), weight.reshape(count, rows, lanes), first, second)
    return new_weight.reshape(count * rows, lanes), new_first, new_second


def halves(levels):
    first = -(-levels // 16) * 8
    return ((0, first), (first, levels))


def column_kernel(
    sizes, theta_hbm, seed_hbm, zonal_hbm, merid_hbm, updraft_hbm, weight_ref,
    out_hbm, grad_ref,
    v, zonal, merid, updraft, edge_x, halo_x, edge_y, halo_y, edge_z, halo_z,
    theta_own, theta_far, profile, back_far, d_in, d_far, w_out, w_in, w_in_t,
    load_sems, seed_sems, theta_sems, x_sems, y_sems, z_sems, back_sems, d_sems, out_sems,
):
    cols, secs, _ = sizes
    levels, rows, lanes = seed_hbm.shape
    slot = v.shape[1]
    pieces = lanes // 128
    half = rows // 2
    col, sec, lev = (lax.axis_index(axis) for axis in REDUCED)
    other = 1 - lev
    own_row = pl.multiple_of(lev * half, half)
    far_row = pl.multiple_of(other * half, half)
    own_slot = lev * slot
    far_slot = other * slot
    parts = halves(levels)
    col_before = lax.rem(col + cols - 1, cols)
    col_after = lax.rem(col + 1, cols)

    theta_in = pltpu.make_async_copy(
        theta_hbm.at[:, pl.ds(own_row, half), :], theta_own, theta_sems.at[0]
    )
    loads, seeds = [], []
    for part, (low, high) in enumerate(parts):
        span = pl.ds(low, high - low)
        loads.append([
            pltpu.make_async_copy(source.at[span], target.at[span], load_sems.at[at, part])
            for at, (source, target) in enumerate(
                ((zonal_hbm, zonal), (merid_hbm, merid), (updraft_hbm, updraft))
            )
        ])
        seeds.append([
            pltpu.make_async_copy(
                seed_hbm.at[span, :, pl.ds(128 * piece, 128)], v.at[piece, span],
                seed_sems.at[piece, part],
            )
            for piece in range(pieces)
        ])
    for group in seeds + loads:
        for copy in group:
            copy.start()
    theta_in.start()

    barrier = pltpu.get_barrier_semaphore()
    pl.semaphore_signal(barrier, inc=1, device_id={"col": col_before}, device_id_type=MESH)
    pl.semaphore_signal(barrier, inc=1, device_id={"col": col_after}, device_id_type=MESH)
    pl.semaphore_signal(barrier, inc=1, device_id={"lev": other}, device_id_type=MESH)

    @pl.when(sec > 0)
    def _():
        pl.semaphore_signal(barrier, inc=1, device_id={"sec": sec - 1}, device_id_type=MESH)

    @pl.when(sec < secs - 1)
    def _():
        pl.semaphore_signal(barrier, inc=1, device_id={"sec": sec + 1}, device_id_type=MESH)

    @pl.when(sec == secs - 1)
    def _():
        halo_y[...] = jnp.zeros_like(halo_y)

    @pl.when(lev == 1)
    def _():
        halo_z[...] = jnp.zeros_like(halo_z)

    pl.semaphore_wait(
        barrier, 3 + (sec > 0).astype(jnp.int32) + (sec < secs - 1).astype(jnp.int32)
    )

    theta_out = pltpu.make_async_remote_copy(
        src_ref=theta_hbm.at[:, pl.ds(far_row, half), :], dst_ref=theta_far,
        send_sem=theta_sems.at[1], recv_sem=theta_sems.at[2],
        device_id={"lev": other}, device_id_type=MESH,
    )
    theta_out.start()

    def x_copy(step, part):
        low, high = parts[part]
        span = pl.ds(low, slot - low if part else high)
        return pltpu.make_async_remote_copy(
            src_ref=edge_x.at[step, span], dst_ref=halo_x.at[step, span],
            send_sem=x_sems.at[0, step, part], recv_sem=x_sems.at[1, step, part],
            device_id={"col": col_before}, device_id_type=MESH,
        )

    def y_copy(step, part):
        return pltpu.make_async_remote_copy(
            src_ref=edge_y.at[step, part], dst_ref=halo_y.at[step, part],
            send_sem=y_sems.at[0, step, part], recv_sem=y_sems.at[1, step, part],
            device_id={"sec": jnp.maximum(sec - 1, 0)}, device_id_type=MESH,
        )

    def z_copy(step):
        return pltpu.make_async_remote_copy(
            src_ref=edge_z.at[step], dst_ref=halo_z.at[step],
            send_sem=z_sems.at[0, step], recv_sem=z_sems.at[1, step],
            device_id={"lev": 0}, device_id_type=MESH,
        )

    def back_copy(part):
        low, high = parts[part]
        span = pl.ds(low, high - low)
        return pltpu.make_async_remote_copy(
            src_ref=v.at[:, span, pl.ds(far_row, half), :], dst_ref=back_far.at[:, span],
            send_sem=back_sems.at[0, part], recv_sem=back_sems.at[1, part],
            device_id={"lev": other}, device_id_type=MESH,
        )

    def whole(ref, z, span=slice(None)):
        return jnp.concatenate([ref[piece, z, span, :] for piece in range(pieces)], axis=1)

    def lay(ref, z, value):
        for piece in range(pieces):
            ref[piece, z] = value[:, 128 * piece : 128 * piece + 128]

    tiles = rows // 8
    lane = lax.broadcasted_iota(jnp.int32, (8, 128), 1)
    last_lane = lax.broadcasted_iota(jnp.int32, (rows, lanes), 1) == lanes - 1
    last_row = lax.broadcasted_iota(jnp.int32, (rows, lanes), 0) == rows - 1

    def keep_edges(value, z, low, step, packed):
        edge_x[step, pl.ds(z, 1), :] = value[0:1]
        for tile in range(tiles):
            packed = jnp.where(
                lane == (z - low) * tiles + tile, value[8 * tile : 8 * tile + 8, 0:1], packed
            )
        return packed

    def send_edges(step, part, packed):
        edge_y[step, part] = packed
        x_copy(step, part).start()

        @pl.when(sec > 0)
        def _():
            y_copy(step, part).start()

        if part == 0:
            edge_z[step] = whole(v, 0)

            @pl.when(lev == 1)
            def _():
                z_copy(step).start()

    def advance(z, low, step, part, above):
        now = whole(v, z)
        strip = pltpu.roll(halo_y[step, part], lax.rem(128 - (z - low) * tiles, 128), axis=1)
        column = jnp.concatenate([strip[:, tile : tile + 1] for tile in range(tiles)], axis=0)
        next_x = jnp.where(last_row, halo_x[step, pl.ds(z, 1), :], pltpu.roll(now, rows - 1, axis=0))
        next_y = jnp.where(last_lane, column, pltpu.roll(now, lanes - 1, axis=1))
        new = (
            now + zonal[z] * (next_x - now) + merid[z] * (next_y - now) + updraft[z] * (above - now)
        )
        lay(v, z, new)
        return new

    nothing = jnp.zeros((8, 128), jnp.float32)
    for part, (low, high) in enumerate(parts):
        for copy in seeds[part]:
            copy.wait()
        packed = lax.fori_loop(
            low, high, lambda z, packed: keep_edges(whole(v, z), z, low, 0, packed), nothing
        )
        send_edges(0, part, packed)

    weights = weight_ref[...]
    middle = weights.shape[1] // 2
    w_out[...] = weights[:, :middle].astype(jnp.bfloat16)
    w_in[...] = weights[:, middle:].astype(jnp.bfloat16)
    w_in_t[...] = weights[:, middle:].T.astype(jnp.bfloat16)
    v[:, levels:] = jnp.zeros((pieces, slot - levels, rows, 128), jnp.float32)
    back_far[:, levels:] = jnp.zeros((pieces, slot - levels, half, 128), jnp.float32)
    for start in (levels, slot + levels):
        profile[:, start : start + slot - levels] = jnp.zeros(
            (pieces, slot - levels, half, 128), jnp.float32
        )
    theta_in.wait()

    def widen(source, first):
        def body(z, carry):
            lay(profile, first + z, source[z].astype(jnp.float32))
            return carry
        lax.fori_loop(0, levels, body, 0)

    widen(theta_own, own_slot)

    for step in range(STEPS):
        for part, (low, high) in enumerate(parts):
            if step == 0:
                for copy in loads[part]:
                    copy.wait()
            x_copy(step, part).wait_recv()

            @pl.when(sec < secs - 1)
            def _():
                y_copy(step, part).wait_recv()

            more = step + 1 < STEPS
            inner = high if part == 0 else high - 1

            def body(z, packed):
                new = advance(z, low, step, part, whole(v, z + 1))
                return keep_edges(new, z, low, step + 1, packed) if more else packed

            packed = lax.fori_loop(low, inner, body, nothing)
            if part == 1:

                @pl.when(lev == 0)
                def _():
                    z_copy(step).wait_recv()

                new = advance(inner, low, step, part, halo_z[step])
                if more:
                    packed = keep_edges(new, inner, low, step + 1, packed)
            if more:
                send_edges(step + 1, part, packed)
            else:
                back_copy(part).start()

    theta_out.wait_recv()
    widen(theta_far, far_slot)
    for part in range(2):
        back_copy(part).wait_recv()

    grad_ref[...] = jnp.zeros_like(grad_ref)
    v_rows = v.reshape(pieces * slot * rows, 128)
    far_rows = back_far.reshape(pieces * slot * half, 128)
    profile_rows = profile.reshape(pieces * 2 * slot * half, 128)
    d_rows = d_in.reshape(pieces * 2 * slot * half, 128)
    chunk, batch = 8, 4
    places = [(row, piece) for row in range(batch) for piece in range(pieces)]

    def d_copy(at):
        span = pl.ds(pl.multiple_of(at * chunk, chunk), chunk)
        return pltpu.make_async_remote_copy(
            src_ref=d_in.at[:, pl.ds(far_slot, levels), span, :],
            dst_ref=d_far.at[:, :, span, :],
            send_sem=d_sems.at[0, at], recv_sem=d_sems.at[1, at],
            device_id={"lev": other}, device_id_type=MESH,
        )

    def out_copy(at, side):
        first = own_row if side == 0 else far_row
        span = pl.ds(pl.multiple_of(first + at * chunk, chunk), chunk)
        return pltpu.make_async_copy(
            zonal.at[:, span, :], out_hbm.at[:, span, :], out_sems.at[side, at]
        )

    nt = (((1,), (1,)), ((), ()))

    def network(at, carry):
        for sub in range(chunk // batch):
            first = at * chunk + sub * batch
            x_parts, b_parts = [], []
            for row, piece in places:
                r = first + row
                x_parts.append(
                    profile_rows[pl.ds(piece * 2 * slot * half + r, 2 * slot, stride=half), :].astype(jnp.bfloat16)
                )
                own = v_rows[pl.ds(piece * slot * rows + own_row + r, slot, stride=rows), :]
                far = far_rows[pl.ds(piece * slot * half + r, slot, stride=half), :]
                low_half = jnp.where(lev == 0, own, far)
                high_half = jnp.where(lev == 0, far, own)
                b_parts.append(
                    jnp.concatenate([low_half, high_half], axis=0).astype(jnp.bfloat16)
                )
            flat = jnp.concatenate(x_parts, axis=1)
            back = jnp.concatenate(b_parts, axis=1)
            act = jnp.tanh(jnp.dot(w_in[...], flat, preferred_element_type=jnp.float32))
            d_act = jnp.dot(w_out[...], back, preferred_element_type=jnp.float32)
            d_pre = (d_act * (1.0 - act * act)).astype(jnp.bfloat16)
            of_out = lax.dot_general(
                act.astype(jnp.bfloat16), back, nt, preferred_element_type=jnp.float32
            )
            of_in = lax.dot_general(d_pre, flat, nt, preferred_element_type=jnp.float32)
            grad_ref[...] += jnp.concatenate([of_out, of_in], axis=1)
            d_input = jnp.dot(w_in_t[...], d_pre, preferred_element_type=jnp.float32)
            d_input = d_input.astype(jnp.bfloat16).astype(jnp.float32)
            for at_place, (row, piece) in enumerate(places):
                start = piece * 2 * slot * half + first + row
                d_rows[pl.ds(start, 2 * slot, stride=half), :] = (
                    d_input[:, at_place * 128 : at_place * 128 + 128]
                )
        d_copy(at).start()
        span = pl.ds(pl.multiple_of(at * chunk, chunk), chunk)
        own_span = pl.ds(pl.multiple_of(own_row + at * chunk, chunk), chunk)

        def body(z, carry):
            zonal[z, own_span, :] = whole(v, z, own_span) + whole(d_in, own_slot + z, span)
            return carry

        lax.fori_loop(0, levels, body, 0, unroll=5 if levels % 5 == 0 else 1)
        out_copy(at, 0).start()
        return carry

    chunks = half // chunk
    lax.fori_loop(0, chunks, network, 0)
    def finish(at, carry):
        d_copy(at).wait_recv()
        span = pl.ds(pl.multiple_of(at * chunk, chunk), chunk)
        far_span = pl.ds(pl.multiple_of(far_row + at * chunk, chunk), chunk)

        def body(z, carry):
            zonal[z, far_span, :] = whole(v, z, far_span) + whole(d_far, z, span)
            return carry

        lax.fori_loop(0, levels, body, 0, unroll=5 if levels % 5 == 0 else 1)
        out_copy(at, 1).start()
        return carry

    lax.fori_loop(0, chunks, finish, 0)

    def drain(at, carry):
        d_copy(at).wait_send()
        out_copy(at, 0).wait()
        out_copy(at, 1).wait()
        return carry

    lax.fori_loop(0, chunks, drain, 0)
    theta_out.wait_send()
    for part in range(2):
        back_copy(part).wait_send()
    for step in range(STEPS):
        for part in range(2):
            x_copy(step, part).wait_send()

            @pl.when(sec > 0)
            def _():
                y_copy(step, part).wait_send()

        @pl.when(lev == 1)
        def _():
            z_copy(step).wait_send()


def columns_back(sizes, theta, seed, zonal, merid, updraft, weight):
    levels, rows, lanes = seed.shape
    hidden, width = weight.shape
    slot, half, pieces = width // 4, rows // 2, lanes // 128
    f32, bf16 = jnp.float32, jnp.bfloat16
    hbm = pl.BlockSpec(memory_space=pl.ANY)
    vmem = pl.BlockSpec(memory_space=pltpu.VMEM)
    dma = pltpu.SemaphoreType.DMA
    ratio = pltpu.VMEM((levels, rows, lanes), f32)
    return pl.pallas_call(
        functools.partial(column_kernel, sizes),
        out_shape=[
            jax.ShapeDtypeStruct((levels, rows, lanes), f32),
            jax.ShapeDtypeStruct((hidden, width), f32),
        ],
        in_specs=[hbm] * 5 + [vmem],
        out_specs=[hbm, vmem],
        scratch_shapes=[
            pltpu.VMEM((pieces, slot, rows, 128), f32), ratio, ratio, ratio,
            pltpu.VMEM((STEPS, slot, lanes), f32), pltpu.VMEM((STEPS, slot, lanes), f32),
            pltpu.VMEM((STEPS, 2, 8, 128), f32), pltpu.VMEM((STEPS, 2, 8, 128), f32),
            pltpu.VMEM((STEPS, rows, lanes), f32), pltpu.VMEM((STEPS, rows, lanes), f32),
            pltpu.VMEM((levels, half, lanes), bf16), pltpu.VMEM((levels, half, lanes), bf16),
            pltpu.VMEM((pieces, 2 * slot, half, 128), f32),
            pltpu.VMEM((pieces, slot, half, 128), f32),
            pltpu.VMEM((pieces, 2 * slot, half, 128), f32),
            pltpu.VMEM((pieces, levels, half, 128), f32),
            pltpu.VMEM((hidden, width // 2), bf16), pltpu.VMEM((hidden, width // 2), bf16),
            pltpu.VMEM((width // 2, hidden), bf16),
            dma((3, 2)), dma((pieces, 2)), dma((3,)), dma((2, STEPS, 2)), dma((2, STEPS, 2)), dma((2, STEPS)),
            dma((2, 2)), dma((2, half // 8)), dma((2, half // 8)),
        ],
        compiler_params=pltpu.CompilerParams(
            collective_id=2, has_side_effects=True, vmem_limit_bytes=48 * 1024 * 1024
        ),
        name="columns_back",
    )(theta, seed, zonal, merid, updraft, weight)


def shards(
    thermal_departure,
    seed_sensitivity,
    zonal_flow_ratio,
    meridional_flow_ratio,
    updraft_flow_ratio,
    entry_layer_matrix,
    final_layer_matrix,
    mean_estimate_entry_matrix,
    squared_estimate_entry_matrix,
    mean_estimate_final_matrix,
    squared_estimate_final_matrix,
):
    levels_all = entry_layer_matrix.shape[0]
    total_cols = (
        seed_sensitivity.shape[1]
        * seed_sensitivity.shape[2]
        * lax.axis_size("col")
        * lax.axis_size("sec")
    )
    factor = 1.0 / math.sqrt(total_cols)
    sizes = tuple(lax.axis_size(axis) for axis in REDUCED)
    levs = sizes[2]

    def packed(of_out, of_in):
        return jnp.concatenate([slots(of_out, levs), slots(of_in.T, levs)], axis=1)

    def unpacked(value):
        half = value.shape[1] // 2
        return (
            unslots(value[:, half:], levs, levels_all).T,
            unslots(value[:, :half], levs, levels_all),
        )

    weight = packed(final_layer_matrix, entry_layer_matrix)
    input_cotangent, grad = columns_back(
        sizes, thermal_departure, seed_sensitivity, zonal_flow_ratio, meridional_flow_ratio,
        updraft_flow_ratio, weight,
    )
    new_weight, new_first, new_second = reduce_update(
        sizes, factor, grad, weight,
        packed(mean_estimate_final_matrix, mean_estimate_entry_matrix),
        packed(squared_estimate_final_matrix, squared_estimate_entry_matrix),
    )
    new_w_in, new_w_out = unpacked(new_weight)
    new_first_in, new_first_out = unpacked(new_first)
    new_second_in, new_second_out = unpacked(new_second)
    return (
        input_cotangent,
        new_w_in,
        new_w_out,
        new_first_in,
        new_second_in,
        new_first_out,
        new_second_out,
    )


def solution(mesh):
    in_specs = (
        P("lev", ("group", "col"), "sec"),
        P("lev", ("group", "col"), "sec"),
        P("lev", ("group", "col"), "sec"),
        P("lev", ("group", "col"), "sec"),
        P("lev", ("group", "col"), "sec"),
        P(),
        P(),
        P(None, ("col", "sec", "lev")),
        P(None, ("col", "sec", "lev")),
        P(("col", "sec", "lev"), None),
        P(("col", "sec", "lev"), None),
    )
    out_specs = (
        P("lev", ("group", "col"), "sec"),
        P("group", None),
        P("group", None),
        P("group", ("col", "sec", "lev")),
        P("group", ("col", "sec", "lev")),
        P(("group", "col", "sec", "lev"), None),
        P(("group", "col", "sec", "lev"), None),
    )
    return jax.shard_map(shards, mesh=mesh, in_specs=in_specs, out_specs=out_specs, check_vma=False)
```

```python
import functools
import math

import jax
import jax.numpy as jnp
from jax import lax
from jax.experimental import pallas as pl
from jax.experimental.pallas import tpu as pltpu
from jax.sharding import PartitionSpec as P

STEPS = 4
GROUP = 4


bias_first = 1.0 - 0.9**10
bias_second = 1.0 - 0.999**10


def adam_update(weight, grad, first, second):
    new_first = 0.9 * first + 0.1 * grad
    new_second = 0.999 * second + 0.001 * grad * grad
    step_size = new_first / bias_first / (jnp.sqrt(new_second / bias_second) + 1e-08)
    return (weight - 0.01 * step_size, new_first, new_second)


MESH = pl.DeviceIdType.MESH
REDUCED = ("col", "sec", "lev")


def slot_size(levels):
    return -(-levels // 8) * 8


def peer_at(position, sizes):
    _, secs, levs = sizes
    return {
        "col": lax.div(position, secs * levs),
        "sec": lax.rem(lax.div(position, levs), secs),
        "lev": lax.rem(position, levs),
    }


def own_position(sizes):
    _, secs, levs = sizes
    return (lax.axis_index("col") * secs + lax.axis_index("sec")) * levs + lax.axis_index("lev")


def exchange(
    sizes, factor, grad_ref, own_share, gathered, landed, piece,
    send_sems, recv_sems, out_sems, in_sems,
):
    count = sizes[0] * sizes[1] * sizes[2]
    me = own_position(sizes)
    barrier = pltpu.get_barrier_semaphore()

    def greet(hop, carry):
        peer = lax.rem(me + hop, count)
        pl.semaphore_signal(barrier, inc=1, device_id=peer_at(peer, sizes), device_id_type=MESH)
        return carry

    lax.fori_loop(1, count, greet, 0)
    pl.semaphore_wait(barrier, count - 1)

    def share(hop):
        peer = lax.rem(me + hop, count)
        return pltpu.make_async_remote_copy(
            src_ref=grad_ref.at[peer], dst_ref=landed.at[hop],
            send_sem=send_sems.at[hop], recv_sem=recv_sems.at[hop],
            device_id=peer_at(peer, sizes), device_id_type=MESH,
        )

    def spread(hop):
        peer = lax.rem(me + hop, count)
        return pltpu.make_async_remote_copy(
            src_ref=piece, dst_ref=gathered.at[me],
            send_sem=out_sems.at[hop], recv_sem=in_sems.at[hop],
            device_id=peer_at(peer, sizes), device_id_type=MESH,
        )

    def start(make):
        def body(hop, carry):
            make(hop).start()
            return carry
        lax.fori_loop(1, count, body, 0)

    start(share)
    weight, first, second = own_share(me)

    def add(hop, total):
        share(hop).wait_recv()
        return total + landed[hop]

    total = lax.fori_loop(1, count, add, grad_ref[me])
    new, new_first, new_second = adam_update(weight, total * factor, first, second)
    piece[...] = new
    start(spread)
    gathered[me] = new

    def leave(hop, carry):
        share(hop).wait_send()
        return carry

    def arrive(hop, carry):
        spread(hop).wait_recv()
        spread(hop).wait_send()
        return carry

    lax.fori_loop(1, count, leave, 0)
    return new_first, new_second, lambda: lax.fori_loop(1, count, arrive, 0)


def reduce_kernel(
    sizes, factor, grad_ref, w_in_ref, w_out_ref, first_in, second_in, first_out, second_out,
    new_w_in, new_w_out, new_first_in, new_second_in, new_first_out, new_second_out,
    gathered, landed, piece, wide, tall, few, turned, *sems,
):
    levels, hidden = w_in_ref.shape
    rows, lanes = piece.shape
    middle = lanes // 2

    def packed(of_in, of_out):
        few[...] = jnp.zeros_like(few)
        few[:, :levels] = of_out[...]
        turned[...] = jnp.zeros_like(turned)
        turned[middle : middle + levels, :rows] = of_in[...]
        return few[...] + turned[...].T[:rows]

    def own_share(me):
        tall[...] = jnp.zeros_like(tall)
        tall[middle : middle + levels] = w_in_ref[...]
        wide[...] = jnp.zeros_like(wide)
        wide[:, :levels] = w_out_ref[...]
        wide[...] = wide[...] + tall[...].T
        weight = wide[pl.ds(pl.multiple_of(me * rows, rows), rows), :]
        return weight, packed(first_in, first_out), packed(second_in, second_out)

    def unpack(value, of_in, of_out):
        of_out[...] = value[:, :levels]
        turned[:rows] = value
        of_in[...] = turned[...].T[middle : middle + levels, :rows]

    new_first, new_second, arrive = exchange(
        sizes, factor, grad_ref, own_share, gathered, landed, piece, *sems
    )
    unpack(new_first, new_first_in, new_first_out)
    unpack(new_second, new_second_in, new_second_out)
    arrive()
    weights = gathered[...].reshape(hidden, lanes)
    new_w_out[...] = weights[:, :levels]
    new_w_in[...] = weights.T[middle : middle + levels]


def narrow_kernel(
    sizes, factor, grad_ref, weight_ref, first_ref, second_ref,
    gathered, new_first_ref, new_second_ref, landed, piece, *sems,
):
    new_first_ref[...], new_second_ref[...], arrive = exchange(
        sizes, factor, grad_ref, lambda me: (weight_ref[me], first_ref[...], second_ref[...]),
        gathered, landed, piece, *sems,
    )
    arrive()


def reduce_update(sizes, factor, grad, w_in, w_out, first_in, second_in, first_out, second_out):
    count = sizes[0] * sizes[1] * sizes[2]
    levels, hidden = w_in.shape
    lanes = grad.shape[1]
    rows, middle = hidden // count, lanes // 2
    f32 = jnp.float32
    vmem = pl.BlockSpec(memory_space=pltpu.VMEM)
    shares = (count, rows, lanes)
    sems = [pltpu.SemaphoreType.DMA((count,))] * 4
    grad = grad.reshape(shares)

    def call(kernel, shapes, scratch, args):
        return pl.pallas_call(
            functools.partial(kernel, sizes, factor),
            out_shape=[jax.ShapeDtypeStruct(shape, f32) for shape in shapes],
            in_specs=[vmem] * len(args),
            out_specs=[vmem] * len(shapes),
            scratch_shapes=[pltpu.VMEM(shape, f32) for shape in scratch] + sems,
            compiler_params=pltpu.CompilerParams(collective_id=1, has_side_effects=True),
            name="reduce_update",
        )(*args)

    if rows % 8 == 0 and rows <= lanes:
        return call(
            reduce_kernel,
            [w_in.shape, w_out.shape, (levels, rows), (levels, rows), (rows, levels), (rows, levels)],
            [shares, shares, (rows, lanes), (hidden, lanes), (lanes, hidden), (rows, lanes),
             (lanes, lanes)],
            (grad, w_in, w_out, first_in, second_in, first_out, second_out),
        )

    def packed(of_in, of_out):
        pad = ((0, 0), (0, middle - levels))
        return jnp.concatenate([jnp.pad(of_out, pad), jnp.pad(of_in.T, pad)], axis=1)

    def unpacked(value):
        return value[:, middle : middle + levels].T, value[:, :levels]

    weight, first, second = call(
        narrow_kernel, [shares, (rows, lanes), (rows, lanes)], [shares, (rows, lanes)],
        (grad, packed(w_in, w_out).reshape(shares), packed(first_in, first_out),
         packed(second_in, second_out)),
    )
    of_in, of_out = zip(*map(unpacked, (weight.reshape(hidden, lanes), first, second)))
    return of_in[0], of_out[0], of_in[1], of_in[2], of_out[1], of_out[2]


def halves(levels):
    first = -(-levels // 16) * 8
    return ((0, first), (first, levels))


def column_kernel(
    sizes, theta_hbm, seed_hbm, zonal_hbm, merid_hbm, updraft_hbm, w_in_ref, w_out_ref,
    out_hbm, grad_ref,
    v, zonal, merid, updraft, edge_x, halo_x, edge_y, halo_y, edge_z, halo_z,
    theta_own, theta_far, profile, back_far, d_in, d_far, w_out, w_in, w_in_t, wide, tall,
    load_sems, seed_sems, theta_sems, x_sems, y_sems, z_sems, back_sems, d_sems, out_sems,
):
    cols, secs, _ = sizes
    levels, rows, lanes = seed_hbm.shape
    slot = v.shape[1]
    pieces = lanes // 128
    half = rows // 2
    col, sec, lev = (lax.axis_index(axis) for axis in REDUCED)
    other = 1 - lev
    own_row = pl.multiple_of(lev * half, half)
    far_row = pl.multiple_of(other * half, half)
    own_slot = lev * slot
    far_slot = other * slot
    parts = halves(levels)
    col_before = lax.rem(col + cols - 1, cols)
    col_after = lax.rem(col + 1, cols)

    theta_in = pltpu.make_async_copy(
        theta_hbm.at[:, pl.ds(own_row, half), :], theta_own, theta_sems.at[0]
    )
    loads, seeds = [], []
    for part, (low, high) in enumerate(parts):
        span = pl.ds(low, high - low)
        loads.append([
            pltpu.make_async_copy(source.at[span], target.at[span], load_sems.at[at, part])
            for at, (source, target) in enumerate(
                ((zonal_hbm, zonal), (merid_hbm, merid), (updraft_hbm, updraft))
            )
        ])
        seeds.append([
            pltpu.make_async_copy(
                seed_hbm.at[span, :, pl.ds(128 * piece, 128)], v.at[piece, span],
                seed_sems.at[piece, part],
            )
            for piece in range(pieces)
        ])
    for group in seeds + loads:
        for copy in group:
            copy.start()
    theta_in.start()

    barrier = pltpu.get_barrier_semaphore()
    pl.semaphore_signal(barrier, inc=1, device_id={"col": col_before}, device_id_type=MESH)
    pl.semaphore_signal(barrier, inc=1, device_id={"col": col_after}, device_id_type=MESH)
    pl.semaphore_signal(barrier, inc=1, device_id={"lev": other}, device_id_type=MESH)

    @pl.when(sec > 0)
    def _():
        pl.semaphore_signal(barrier, inc=1, device_id={"sec": sec - 1}, device_id_type=MESH)

    @pl.when(sec < secs - 1)
    def _():
        pl.semaphore_signal(barrier, inc=1, device_id={"sec": sec + 1}, device_id_type=MESH)

    @pl.when(sec == secs - 1)
    def _():
        halo_y[...] = jnp.zeros_like(halo_y)

    @pl.when(lev == 1)
    def _():
        halo_z[...] = jnp.zeros_like(halo_z)

    pl.semaphore_wait(
        barrier, 3 + (sec > 0).astype(jnp.int32) + (sec < secs - 1).astype(jnp.int32)
    )

    theta_out = pltpu.make_async_remote_copy(
        src_ref=theta_hbm.at[:, pl.ds(far_row, half), :], dst_ref=theta_far,
        send_sem=theta_sems.at[1], recv_sem=theta_sems.at[2],
        device_id={"lev": other}, device_id_type=MESH,
    )
    theta_out.start()

    def x_copy(step, part):
        low, high = parts[part]
        span = pl.ds(low, slot - low if part else high)
        return pltpu.make_async_remote_copy(
            src_ref=edge_x.at[step, span], dst_ref=halo_x.at[step, span],
            send_sem=x_sems.at[0, step, part], recv_sem=x_sems.at[1, step, part],
            device_id={"col": col_before}, device_id_type=MESH,
        )

    def y_copy(step, part):
        return pltpu.make_async_remote_copy(
            src_ref=edge_y.at[step, part], dst_ref=halo_y.at[step, part],
            send_sem=y_sems.at[0, step, part], recv_sem=y_sems.at[1, step, part],
            device_id={"sec": jnp.maximum(sec - 1, 0)}, device_id_type=MESH,
        )

    def z_copy(step):
        return pltpu.make_async_remote_copy(
            src_ref=edge_z.at[step], dst_ref=halo_z.at[step],
            send_sem=z_sems.at[0, step], recv_sem=z_sems.at[1, step],
            device_id={"lev": 0}, device_id_type=MESH,
        )

    def back_copy(part):
        low, high = parts[part]
        span = pl.ds(low, high - low)
        return pltpu.make_async_remote_copy(
            src_ref=v.at[:, span, pl.ds(far_row, half), :], dst_ref=back_far.at[:, span],
            send_sem=back_sems.at[0, part], recv_sem=back_sems.at[1, part],
            device_id={"lev": other}, device_id_type=MESH,
        )

    def whole(ref, z, span=slice(None)):
        return jnp.concatenate([ref[piece, z, span, :] for piece in range(pieces)], axis=1)

    def lay(ref, z, value):
        for piece in range(pieces):
            ref[piece, z] = value[:, 128 * piece : 128 * piece + 128]

    tiles = rows // 8
    lane = lax.broadcasted_iota(jnp.int32, (8, 128), 1)
    last_lane = lax.broadcasted_iota(jnp.int32, (rows, 128), 1) == 127
    last_row = lax.broadcasted_iota(jnp.int32, (rows, lanes), 0) == rows - 1

    def keep_edges(value, z, low, step, packed):
        edge_x[step, pl.ds(z, 1), :] = value[0:1]
        for tile in range(tiles):
            packed = jnp.where(
                lane == (z - low) * tiles + tile, value[8 * tile : 8 * tile + 8, 0:1], packed
            )
        return packed

    def send_edges(step, part, packed):
        edge_y[step, part] = packed
        x_copy(step, part).start()

        @pl.when(sec > 0)
        def _():
            y_copy(step, part).start()

        if part == 0:
            edge_z[step] = whole(v, 0)

            @pl.when(lev == 1)
            def _():
                z_copy(step).start()

    def advance(first, count, low, step, part, packed, above=None):
        levels_now = [whole(v, first + at) for at in range(count)]
        levels_now.append(whole(v, first + count) if above is None else above)
        strip = halo_y[step, part]
        news = []
        for at in range(count):
            z, now, over = first + at, levels_now[at], levels_now[at + 1]
            side = jnp.concatenate([
                pltpu.roll(strip, lax.rem(255 - (z - low) * tiles - tile, 128), axis=1)
                for tile in range(tiles)
            ], axis=0)
            next_x = jnp.where(
                last_row, halo_x[step, pl.ds(z, 1), :], pltpu.roll(now, rows - 1, axis=0)
            )
            shifted = pltpu.roll(now, lanes - 1, axis=1)
            next_y = jnp.concatenate([
                shifted[:, : lanes - 128], jnp.where(last_lane, side, shifted[:, lanes - 128 :])
            ], axis=1)
            news.append(
                now + zonal[z] * (next_x - now) + merid[z] * (next_y - now)
                + updraft[z] * (over - now)
            )
        for at, new in enumerate(news):
            lay(v, first + at, new)
            if step + 1 < STEPS:
                packed = keep_edges(new, first + at, low, step + 1, packed)
        return packed

    nothing = jnp.zeros((8, 128), jnp.float32)
    for part, (low, high) in enumerate(parts):
        for copy in seeds[part]:
            copy.wait()
        packed = lax.fori_loop(
            low, high, lambda z, packed: keep_edges(whole(v, z), z, low, 0, packed), nothing
        )
        send_edges(0, part, packed)

    wide[...] = jnp.zeros_like(wide)
    wide[:, : 2 * levels] = w_out_ref[...]
    across = lax.broadcasted_iota(jnp.int32, wide.shape, 1)
    by_slot = jnp.where(across < levels, wide[...], pltpu.roll(wide[...], slot - levels, axis=1))
    w_out[...] = by_slot[:, : 2 * slot].astype(jnp.bfloat16)
    tall[...] = jnp.zeros_like(tall)
    tall[0:levels] = w_in_ref[0:levels]
    tall[slot : slot + levels] = w_in_ref[levels:]
    w_in_t[...] = tall[...].astype(jnp.bfloat16)
    w_in[...] = tall[...].T.astype(jnp.bfloat16)
    v[:, levels:] = jnp.zeros((pieces, slot - levels, rows, 128), jnp.float32)
    back_far[:, levels:] = jnp.zeros((pieces, slot - levels, half, 128), jnp.float32)
    for start in (levels, slot + levels):
        profile[:, start : start + slot - levels] = jnp.zeros(
            (pieces, slot - levels, half, 128), jnp.float32
        )
    theta_in.wait()

    def widen(source, first):
        def body(z, carry):
            lay(profile, first + z, source[z].astype(jnp.float32))
            return carry
        lax.fori_loop(0, levels, body, 0)

    widen(theta_own, own_slot)

    for step in range(STEPS):
        for part, (low, high) in enumerate(parts):
            if step == 0:
                for copy in loads[part]:
                    copy.wait()
            x_copy(step, part).wait_recv()

            @pl.when(sec < secs - 1)
            def _():
                y_copy(step, part).wait_recv()

            more = step + 1 < STEPS
            groups = (high - low - (GROUP if part else 0)) // GROUP
            left = high - low - groups * GROUP

            def body(at, packed):
                return advance(low + at * GROUP, GROUP, low, step, part, packed)

            packed = lax.fori_loop(0, groups, body, nothing)
            if part == 1:

                @pl.when(lev == 0)
                def _():
                    z_copy(step).wait_recv()

            if left:
                packed = advance(
                    high - left, left, low, step, part, packed, halo_z[step] if part else None
                )
            if more:
                send_edges(step + 1, part, packed)
            else:
                back_copy(part).start()

    theta_out.wait_recv()
    widen(theta_far, far_slot)
    for part in range(2):
        back_copy(part).wait_recv()

    grad_ref[...] = jnp.zeros_like(grad_ref)
    v_rows = v.reshape(pieces * slot * rows, 128)
    far_rows = back_far.reshape(pieces * slot * half, 128)
    profile_rows = profile.reshape(pieces * 2 * slot * half, 128)
    d_rows = d_in.reshape(pieces * 2 * slot * half, 128)
    chunk, batch = 8, 4
    places = [(row, piece) for row in range(batch) for piece in range(pieces)]

    def d_copy(at):
        span = pl.ds(pl.multiple_of(at * chunk, chunk), chunk)
        return pltpu.make_async_remote_copy(
            src_ref=d_in.at[:, pl.ds(far_slot, levels), span, :],
            dst_ref=d_far.at[:, :, span, :],
            send_sem=d_sems.at[0, at], recv_sem=d_sems.at[1, at],
            device_id={"lev": other}, device_id_type=MESH,
        )

    def out_copy(at, side):
        first = own_row if side == 0 else far_row
        span = pl.ds(pl.multiple_of(first + at * chunk, chunk), chunk)
        return pltpu.make_async_copy(
            zonal.at[:, span, :], out_hbm.at[:, span, :], out_sems.at[side, at]
        )

    nt = (((1,), (1,)), ((), ()))

    def network(at, carry):
        for sub in range(chunk // batch):
            first = at * chunk + sub * batch
            x_parts, b_parts = [], []
            for row, piece in places:
                r = first + row
                x_parts.append(
                    profile_rows[pl.ds(piece * 2 * slot * half + r, 2 * slot, stride=half), :].astype(jnp.bfloat16)
                )
                own = v_rows[pl.ds(piece * slot * rows + own_row + r, slot, stride=rows), :]
                far = far_rows[pl.ds(piece * slot * half + r, slot, stride=half), :]
                low_half = jnp.where(lev == 0, own, far)
                high_half = jnp.where(lev == 0, far, own)
                b_parts.append(
                    jnp.concatenate([low_half, high_half], axis=0).astype(jnp.bfloat16)
                )
            flat = jnp.concatenate(x_parts, axis=1)
            back = jnp.concatenate(b_parts, axis=1)
            act = jnp.tanh(jnp.dot(w_in[...], flat, preferred_element_type=jnp.float32))
            d_act = jnp.dot(w_out[...], back, preferred_element_type=jnp.float32)
            d_pre = (d_act * (1.0 - act * act)).astype(jnp.bfloat16)
            of_out = lax.dot_general(
                act.astype(jnp.bfloat16), back, nt, preferred_element_type=jnp.float32
            )
            of_in = lax.dot_general(d_pre, flat, nt, preferred_element_type=jnp.float32)
            grad_ref[...] += jnp.concatenate([of_out, of_in], axis=1)
            d_input = jnp.dot(w_in_t[...], d_pre, preferred_element_type=jnp.float32)
            d_input = d_input.astype(jnp.bfloat16).astype(jnp.float32)
            for at_place, (row, piece) in enumerate(places):
                start = piece * 2 * slot * half + first + row
                d_rows[pl.ds(start, 2 * slot, stride=half), :] = (
                    d_input[:, at_place * 128 : at_place * 128 + 128]
                )
        d_copy(at).start()
        span = pl.ds(pl.multiple_of(at * chunk, chunk), chunk)
        own_span = pl.ds(pl.multiple_of(own_row + at * chunk, chunk), chunk)

        def body(z, carry):
            zonal[z, own_span, :] = whole(v, z, own_span) + whole(d_in, own_slot + z, span)
            return carry

        lax.fori_loop(0, levels, body, 0, unroll=5 if levels % 5 == 0 else 1)
        out_copy(at, 0).start()
        return carry

    chunks = half // chunk
    lax.fori_loop(0, chunks, network, 0)
    slotted = grad_ref[...]
    at_slot = lax.rem(lax.broadcasted_iota(jnp.int32, slotted.shape, 1), 2 * slot)
    grad_ref[...] = jnp.where(
        at_slot < levels, slotted,
        pltpu.roll(slotted, slotted.shape[1] - (slot - levels), axis=1),
    )

    def finish(at, carry):
        d_copy(at).wait_recv()
        span = pl.ds(pl.multiple_of(at * chunk, chunk), chunk)
        far_span = pl.ds(pl.multiple_of(far_row + at * chunk, chunk), chunk)

        def body(z, carry):
            zonal[z, far_span, :] = whole(v, z, far_span) + whole(d_far, z, span)
            return carry

        lax.fori_loop(0, levels, body, 0, unroll=5 if levels % 5 == 0 else 1)
        out_copy(at, 1).start()
        return carry

    lax.fori_loop(0, chunks, finish, 0)

    def drain(at, carry):
        d_copy(at).wait_send()
        out_copy(at, 0).wait()
        out_copy(at, 1).wait()
        return carry

    lax.fori_loop(0, chunks, drain, 0)
    theta_out.wait_send()
    for part in range(2):
        back_copy(part).wait_send()
    for step in range(STEPS):
        for part in range(2):
            x_copy(step, part).wait_send()

            @pl.when(sec > 0)
            def _():
                y_copy(step, part).wait_send()

        @pl.when(lev == 1)
        def _():
            z_copy(step).wait_send()


def columns_back(sizes, theta, seed, zonal, merid, updraft, weight_in, weight_out):
    levels, rows, lanes = seed.shape
    hidden, width = weight_out.shape[0], 4 * slot_size(levels)
    slot, half, pieces = width // 4, rows // 2, lanes // 128
    f32, bf16 = jnp.float32, jnp.bfloat16
    hbm = pl.BlockSpec(memory_space=pl.ANY)
    vmem = pl.BlockSpec(memory_space=pltpu.VMEM)
    dma = pltpu.SemaphoreType.DMA
    ratio = pltpu.VMEM((levels, rows, lanes), f32)
    return pl.pallas_call(
        functools.partial(column_kernel, sizes),
        out_shape=[
            jax.ShapeDtypeStruct((levels, rows, lanes), f32),
            jax.ShapeDtypeStruct((hidden, width), f32),
        ],
        in_specs=[hbm] * 5 + [vmem] * 2,
        out_specs=[hbm, vmem],
        scratch_shapes=[
            pltpu.VMEM((pieces, slot, rows, 128), f32), ratio, ratio, ratio,
            pltpu.VMEM((STEPS, slot, lanes), f32), pltpu.VMEM((STEPS, slot, lanes), f32),
            pltpu.VMEM((STEPS, 2, 8, 128), f32), pltpu.VMEM((STEPS, 2, 8, 128), f32),
            pltpu.VMEM((STEPS, rows, lanes), f32), pltpu.VMEM((STEPS, rows, lanes), f32),
            pltpu.VMEM((levels, half, lanes), bf16), pltpu.VMEM((levels, half, lanes), bf16),
            pltpu.VMEM((pieces, 2 * slot, half, 128), f32),
            pltpu.VMEM((pieces, slot, half, 128), f32),
            pltpu.VMEM((pieces, 2 * slot, half, 128), f32),
            pltpu.VMEM((pieces, levels, half, 128), f32),
            pltpu.VMEM((hidden, width // 2), bf16), pltpu.VMEM((hidden, width // 2), bf16),
            pltpu.VMEM((width // 2, hidden), bf16),
            pltpu.VMEM((hidden, width), f32), pltpu.VMEM((width // 2, hidden), f32),
            dma((3, 2)), dma((pieces, 2)), dma((3,)), dma((2, STEPS, 2)), dma((2, STEPS, 2)), dma((2, STEPS)),
            dma((2, 2)), dma((2, half // 8)), dma((2, half // 8)),
        ],
        compiler_params=pltpu.CompilerParams(
            collective_id=2, has_side_effects=True, vmem_limit_bytes=48 * 1024 * 1024
        ),
        name="columns_back",
    )(theta, seed, zonal, merid, updraft, weight_in, weight_out)


def shards(
    thermal_departure,
    seed_sensitivity,
    zonal_flow_ratio,
    meridional_flow_ratio,
    updraft_flow_ratio,
    entry_layer_matrix,
    final_layer_matrix,
    mean_estimate_entry_matrix,
    squared_estimate_entry_matrix,
    mean_estimate_final_matrix,
    squared_estimate_final_matrix,
):
    total_cols = (
        seed_sensitivity.shape[1]
        * seed_sensitivity.shape[2]
        * lax.axis_size("col")
        * lax.axis_size("sec")
    )
    factor = 1.0 / math.sqrt(total_cols)
    sizes = tuple(lax.axis_size(axis) for axis in REDUCED)
    input_cotangent, grad = columns_back(
        sizes, thermal_departure, seed_sensitivity, zonal_flow_ratio, meridional_flow_ratio,
        updraft_flow_ratio, entry_layer_matrix, final_layer_matrix,
    )
    return input_cotangent, *reduce_update(
        sizes, factor, grad, entry_layer_matrix, final_layer_matrix,
        mean_estimate_entry_matrix, squared_estimate_entry_matrix,
        mean_estimate_final_matrix, squared_estimate_final_matrix,
    )


def solution(mesh):
    in_specs = (
        P("lev", ("group", "col"), "sec"),
        P("lev", ("group", "col"), "sec"),
        P("lev", ("group", "col"), "sec"),
        P("lev", ("group", "col"), "sec"),
        P("lev", ("group", "col"), "sec"),
        P(),
        P(),
        P(None, ("col", "sec", "lev")),
        P(None, ("col", "sec", "lev")),
        P(("col", "sec", "lev"), None),
        P(("col", "sec", "lev"), None),
    )
    out_specs = (
        P("lev", ("group", "col"), "sec"),
        P("group", None),
        P("group", None),
        P("group", ("col", "sec", "lev")),
        P("group", ("col", "sec", "lev")),
        P(("group", "col", "sec", "lev"), None),
        P(("group", "col", "sec", "lev"), None),
    )
    return jax.shard_map(shards, mesh=mesh, in_specs=in_specs, out_specs=out_specs, check_vma=False)
```

```python
import functools
import math

import jax
import jax.numpy as jnp
from jax import lax
from jax.experimental import pallas as pl
from jax.experimental.pallas import tpu as pltpu
from jax.sharding import PartitionSpec as P

STEPS = 4
GROUP = 4


bias_first = 1.0 - 0.9**10
bias_second = 1.0 - 0.999**10


def adam_update(weight, grad, first, second):
    new_first = 0.9 * first + 0.1 * grad
    new_second = 0.999 * second + 0.001 * grad * grad
    step_size = new_first / bias_first / (jnp.sqrt(new_second / bias_second) + 1e-08)
    return (weight - 0.01 * step_size, new_first, new_second)


MESH = pl.DeviceIdType.MESH
REDUCED = ("col", "sec", "lev")


def slot_size(levels):
    return -(-levels // 8) * 8


def peer_at(position, sizes):
    _, secs, levs = sizes
    return {
        "col": lax.div(position, secs * levs),
        "sec": lax.rem(lax.div(position, levs), secs),
        "lev": lax.rem(position, levs),
    }


def own_position(sizes):
    _, secs, levs = sizes
    return (lax.axis_index("col") * secs + lax.axis_index("sec")) * levs + lax.axis_index("lev")


def exchange(
    sizes, factor, grad_ref, own_share, gathered, landed, piece,
    send_sems, recv_sems, out_sems, in_sems,
):
    count = sizes[0] * sizes[1] * sizes[2]
    me = own_position(sizes)
    barrier = pltpu.get_barrier_semaphore()

    def greet(hop, carry):
        peer = lax.rem(me + hop, count)
        pl.semaphore_signal(barrier, inc=1, device_id=peer_at(peer, sizes), device_id_type=MESH)
        return carry

    lax.fori_loop(1, count, greet, 0)
    pl.semaphore_wait(barrier, count - 1)

    def share(hop):
        peer = lax.rem(me + hop, count)
        return pltpu.make_async_remote_copy(
            src_ref=grad_ref.at[peer], dst_ref=landed.at[hop],
            send_sem=send_sems.at[hop], recv_sem=recv_sems.at[hop],
            device_id=peer_at(peer, sizes), device_id_type=MESH,
        )

    def spread(hop):
        peer = lax.rem(me + hop, count)
        return pltpu.make_async_remote_copy(
            src_ref=piece, dst_ref=gathered.at[me],
            send_sem=out_sems.at[hop], recv_sem=in_sems.at[hop],
            device_id=peer_at(peer, sizes), device_id_type=MESH,
        )

    def start(make):
        def body(hop, carry):
            make(hop).start()
            return carry
        lax.fori_loop(1, count, body, 0)

    start(share)
    weight, first, second = own_share(me)

    def add(hop, total):
        share(hop).wait_recv()
        return total + landed[hop]

    total = lax.fori_loop(1, count, add, grad_ref[me])
    new, new_first, new_second = adam_update(weight, total * factor, first, second)
    piece[...] = new
    start(spread)
    gathered[me] = new

    def leave(hop, carry):
        share(hop).wait_send()
        return carry

    def arrive(hop, carry):
        spread(hop).wait_recv()
        spread(hop).wait_send()
        return carry

    lax.fori_loop(1, count, leave, 0)
    return new_first, new_second, lambda: lax.fori_loop(1, count, arrive, 0)


def reduce_kernel(
    sizes, factor, grad_ref, w_in_ref, w_out_ref, first_in, second_in, first_out, second_out,
    new_w_in, new_w_out, new_first_in, new_second_in, new_first_out, new_second_out,
    gathered, landed, piece, wide, tall, few, *sems,
):
    levels, hidden = w_in_ref.shape
    rows, lanes = piece.shape
    middle = lanes // 2

    def packed(of_in, of_out):
        few[...] = jnp.zeros_like(few)
        few[:, :levels] = of_out[...]
        few[:, middle : middle + levels] = of_in[...]
        return few[...]

    def own_share(me):
        tall[...] = jnp.zeros_like(tall)
        tall[middle : middle + levels] = w_in_ref[...]
        tall[:levels] = w_out_ref[...]
        wide[...] = tall[...].T
        weight = wide[pl.ds(pl.multiple_of(me * rows, rows), rows), :]
        return weight, packed(first_in, first_out), packed(second_in, second_out)

    def unpack(value, of_in, of_out):
        of_out[...] = value[:, :levels]
        of_in[...] = value[:, middle : middle + levels]

    new_first, new_second, arrive = exchange(
        sizes, factor, grad_ref, own_share, gathered, landed, piece, *sems
    )
    unpack(new_first, new_first_in, new_first_out)
    unpack(new_second, new_second_in, new_second_out)
    arrive()
    weights = gathered[...].reshape(hidden, lanes)
    turned = weights.T
    new_w_out[...] = turned[:levels]
    new_w_in[...] = turned[middle : middle + levels]


def narrow_kernel(
    sizes, factor, grad_ref, weight_ref, first_ref, second_ref,
    gathered, new_first_ref, new_second_ref, landed, piece, *sems,
):
    new_first_ref[...], new_second_ref[...], arrive = exchange(
        sizes, factor, grad_ref, lambda me: (weight_ref[me], first_ref[...], second_ref[...]),
        gathered, landed, piece, *sems,
    )
    arrive()


def reduce_update(sizes, factor, grad, w_in, w_out, first_in, second_in, first_out, second_out):
    count = sizes[0] * sizes[1] * sizes[2]
    levels, hidden = w_in.shape
    lanes = grad.shape[1]
    rows, middle = hidden // count, lanes // 2
    f32 = jnp.float32
    vmem = pl.BlockSpec(memory_space=pltpu.VMEM)
    shares = (count, rows, lanes)
    sems = [pltpu.SemaphoreType.DMA((count,))] * 4
    grad = grad.reshape(shares)

    def call(kernel, shapes, scratch, args):
        return pl.pallas_call(
            functools.partial(kernel, sizes, factor),
            out_shape=[jax.ShapeDtypeStruct(shape, f32) for shape in shapes],
            in_specs=[vmem] * len(args),
            out_specs=[vmem] * len(shapes),
            scratch_shapes=[pltpu.VMEM(shape, f32) for shape in scratch] + sems,
            compiler_params=pltpu.CompilerParams(collective_id=1, has_side_effects=True),
            name="reduce_update",
        )(*args)

    if rows % 8 == 0:
        w_in, w_out, m_in, v_in, m_out, v_out = call(
            reduce_kernel,
            [w_in.shape] * 2 + [(rows, levels)] * 4,
            [shares, shares, (rows, lanes), (hidden, lanes), (lanes, hidden), (rows, lanes)],
            (grad, w_in, w_out.T, first_in.T, second_in.T, first_out, second_out),
        )
        return w_in, w_out.T, m_in.T, v_in.T, m_out, v_out

    def packed(of_in, of_out):
        pad = ((0, 0), (0, middle - levels))
        return jnp.concatenate([jnp.pad(of_out, pad), jnp.pad(of_in.T, pad)], axis=1)

    def unpacked(value):
        return value[:, middle : middle + levels].T, value[:, :levels]

    weight, first, second = call(
        narrow_kernel, [shares, (rows, lanes), (rows, lanes)], [shares, (rows, lanes)],
        (grad, packed(w_in, w_out).reshape(shares), packed(first_in, first_out),
         packed(second_in, second_out)),
    )
    of_in, of_out = zip(*map(unpacked, (weight.reshape(hidden, lanes), first, second)))
    return of_in[0], of_out[0], of_in[1], of_in[2], of_out[1], of_out[2]


def halves(levels):
    first = -(-levels // 16) * 8
    return ((0, first), (first, levels))


def column_kernel(
    sizes, theta_hbm, seed_hbm, zonal_hbm, merid_hbm, updraft_hbm, w_in_ref, w_out_ref,
    out_hbm, grad_ref,
    v, zonal, merid, updraft, edge_x, halo_x, edge_y, halo_y, edge_z, halo_z,
    theta_own, theta_far, profile, back_far, d_in, d_far, w_out, w_in, w_in_t, wide, tall,
    load_sems, seed_sems, theta_sems, x_sems, y_sems, z_sems, back_sems, d_sems, out_sems,
):
    cols, secs, _ = sizes
    levels, rows, lanes = seed_hbm.shape
    slot = v.shape[1]
    pieces = lanes // 128
    half = rows // 2
    col, sec, lev = (lax.axis_index(axis) for axis in REDUCED)
    other = 1 - lev
    own_row = pl.multiple_of(lev * half, half)
    far_row = pl.multiple_of(other * half, half)
    own_slot = lev * slot
    far_slot = other * slot
    parts = halves(levels)
    col_before = lax.rem(col + cols - 1, cols)
    col_after = lax.rem(col + 1, cols)

    theta_in = pltpu.make_async_copy(
        theta_hbm.at[:, pl.ds(own_row, half), :], theta_own, theta_sems.at[0]
    )
    loads, seeds = [], []
    for part, (low, high) in enumerate(parts):
        span = pl.ds(low, high - low)
        loads.append([
            pltpu.make_async_copy(source.at[span], target.at[span], load_sems.at[at, part])
            for at, (source, target) in enumerate(
                ((zonal_hbm, zonal), (merid_hbm, merid), (updraft_hbm, updraft))
            )
        ])
        seeds.append([
            pltpu.make_async_copy(
                seed_hbm.at[span, :, pl.ds(128 * piece, 128)], v.at[piece, span],
                seed_sems.at[piece, part],
            )
            for piece in range(pieces)
        ])
    for group in seeds + loads:
        for copy in group:
            copy.start()
    theta_in.start()

    barrier = pltpu.get_barrier_semaphore()
    pl.semaphore_signal(barrier, inc=1, device_id={"col": col_before}, device_id_type=MESH)
    pl.semaphore_signal(barrier, inc=1, device_id={"col": col_after}, device_id_type=MESH)
    pl.semaphore_signal(barrier, inc=1, device_id={"lev": other}, device_id_type=MESH)

    @pl.when(sec > 0)
    def _():
        pl.semaphore_signal(barrier, inc=1, device_id={"sec": sec - 1}, device_id_type=MESH)

    @pl.when(sec < secs - 1)
    def _():
        pl.semaphore_signal(barrier, inc=1, device_id={"sec": sec + 1}, device_id_type=MESH)

    @pl.when(sec == secs - 1)
    def _():
        halo_y[...] = jnp.zeros_like(halo_y)

    @pl.when(lev == 1)
    def _():
        halo_z[...] = jnp.zeros_like(halo_z)

    pl.semaphore_wait(
        barrier, 3 + (sec > 0).astype(jnp.int32) + (sec < secs - 1).astype(jnp.int32)
    )

    theta_out = pltpu.make_async_remote_copy(
        src_ref=theta_hbm.at[:, pl.ds(far_row, half), :], dst_ref=theta_far,
        send_sem=theta_sems.at[1], recv_sem=theta_sems.at[2],
        device_id={"lev": other}, device_id_type=MESH,
    )
    theta_out.start()

    def x_copy(step, part):
        low, high = parts[part]
        span = pl.ds(low, slot - low if part else high)
        return pltpu.make_async_remote_copy(
            src_ref=edge_x.at[step, span], dst_ref=halo_x.at[step, span],
            send_sem=x_sems.at[0, step, part], recv_sem=x_sems.at[1, step, part],
            device_id={"col": col_before}, device_id_type=MESH,
        )

    def y_copy(step, part):
        return pltpu.make_async_remote_copy(
            src_ref=edge_y.at[step, part], dst_ref=halo_y.at[step, part],
            send_sem=y_sems.at[0, step, part], recv_sem=y_sems.at[1, step, part],
            device_id={"sec": jnp.maximum(sec - 1, 0)}, device_id_type=MESH,
        )

    def z_copy(step):
        return pltpu.make_async_remote_copy(
            src_ref=edge_z.at[step], dst_ref=halo_z.at[step],
            send_sem=z_sems.at[0, step], recv_sem=z_sems.at[1, step],
            device_id={"lev": 0}, device_id_type=MESH,
        )

    def back_copy(part):
        low, high = parts[part]
        span = pl.ds(low, high - low)
        return pltpu.make_async_remote_copy(
            src_ref=v.at[:, span, pl.ds(far_row, half), :], dst_ref=back_far.at[:, span],
            send_sem=back_sems.at[0, part], recv_sem=back_sems.at[1, part],
            device_id={"lev": other}, device_id_type=MESH,
        )

    def whole(ref, z, span=slice(None)):
        return jnp.concatenate([ref[piece, z, span, :] for piece in range(pieces)], axis=1)

    def lay(ref, z, value):
        for piece in range(pieces):
            ref[piece, z] = value[:, 128 * piece : 128 * piece + 128]

    tiles = rows // 8
    lane = lax.broadcasted_iota(jnp.int32, (8, 128), 1)
    last_lane = lax.broadcasted_iota(jnp.int32, (rows, 128), 1) == 127
    last_row = lax.broadcasted_iota(jnp.int32, (rows, lanes), 0) == rows - 1

    def keep_edges(value, z, low, step, packed):
        edge_x[step, pl.ds(z, 1), :] = value[0:1]
        for tile in range(tiles):
            packed = jnp.where(
                lane == (z - low) * tiles + tile, value[8 * tile : 8 * tile + 8, 0:1], packed
            )
        return packed

    def send_edges(step, part, packed):
        edge_y[step, part] = packed
        x_copy(step, part).start()

        @pl.when(sec > 0)
        def _():
            y_copy(step, part).start()

        if part == 0:
            edge_z[step] = whole(v, 0)

            @pl.when(lev == 1)
            def _():
                z_copy(step).start()

    def advance(first, count, low, step, part, packed, above=None):
        levels_now = [whole(v, first + at) for at in range(count)]
        levels_now.append(whole(v, first + count) if above is None else above)
        strip = halo_y[step, part]
        news = []
        for at in range(count):
            z, now, over = first + at, levels_now[at], levels_now[at + 1]
            side = jnp.concatenate([
                pltpu.roll(strip, lax.rem(255 - (z - low) * tiles - tile, 128), axis=1)
                for tile in range(tiles)
            ], axis=0)
            next_x = jnp.where(
                last_row, halo_x[step, pl.ds(z, 1), :], pltpu.roll(now, rows - 1, axis=0)
            )
            shifted = pltpu.roll(now, lanes - 1, axis=1)
            next_y = jnp.concatenate([
                shifted[:, : lanes - 128], jnp.where(last_lane, side, shifted[:, lanes - 128 :])
            ], axis=1)
            news.append(
                now + zonal[z] * (next_x - now) + merid[z] * (next_y - now)
                + updraft[z] * (over - now)
            )
        for at, new in enumerate(news):
            lay(v, first + at, new)
            if step + 1 < STEPS:
                packed = keep_edges(new, first + at, low, step + 1, packed)
        return packed

    nothing = jnp.zeros((8, 128), jnp.float32)
    for part, (low, high) in enumerate(parts):
        for copy in seeds[part]:
            copy.wait()
        packed = lax.fori_loop(
            low, high, lambda z, packed: keep_edges(whole(v, z), z, low, 0, packed), nothing
        )
        send_edges(0, part, packed)

    wide[...] = jnp.zeros_like(wide)
    tall[...] = jnp.zeros_like(tall)
    tall[: 2 * levels] = w_out_ref[...]
    wide[:, : 2 * slot] = tall[...].T
    across = lax.broadcasted_iota(jnp.int32, wide.shape, 1)
    by_slot = jnp.where(across < levels, wide[...], pltpu.roll(wide[...], slot - levels, axis=1))
    w_out[...] = by_slot[:, : 2 * slot].astype(jnp.bfloat16)
    tall[...] = jnp.zeros_like(tall)
    tall[0:levels] = w_in_ref[0:levels]
    tall[slot : slot + levels] = w_in_ref[levels:]
    w_in_t[...] = tall[...].astype(jnp.bfloat16)
    w_in[...] = tall[...].T.astype(jnp.bfloat16)
    v[:, levels:] = jnp.zeros((pieces, slot - levels, rows, 128), jnp.float32)
    back_far[:, levels:] = jnp.zeros((pieces, slot - levels, half, 128), jnp.float32)
    for start in (levels, slot + levels):
        profile[:, start : start + slot - levels] = jnp.zeros(
            (pieces, slot - levels, half, 128), jnp.float32
        )
    theta_in.wait()

    def widen(source, first):
        def body(z, carry):
            lay(profile, first + z, source[z].astype(jnp.float32))
            return carry
        lax.fori_loop(0, levels, body, 0)

    widen(theta_own, own_slot)

    for step in range(STEPS):
        for part, (low, high) in enumerate(parts):
            if step == 0:
                for copy in loads[part]:
                    copy.wait()
            x_copy(step, part).wait_recv()

            @pl.when(sec < secs - 1)
            def _():
                y_copy(step, part).wait_recv()

            more = step + 1 < STEPS
            groups = (high - low - (GROUP if part else 0)) // GROUP
            left = high - low - groups * GROUP

            def body(at, packed):
                return advance(low + at * GROUP, GROUP, low, step, part, packed)

            packed = lax.fori_loop(0, groups, body, nothing)
            if part == 1:

                @pl.when(lev == 0)
                def _():
                    z_copy(step).wait_recv()

            if left:
                packed = advance(
                    high - left, left, low, step, part, packed, halo_z[step] if part else None
                )
            if more:
                send_edges(step + 1, part, packed)
            else:
                back_copy(part).start()

    theta_out.wait_recv()
    widen(theta_far, far_slot)
    for part in range(2):
        back_copy(part).wait_recv()

    grad_ref[...] = jnp.zeros_like(grad_ref)
    v_rows = v.reshape(pieces * slot * rows, 128)
    far_rows = back_far.reshape(pieces * slot * half, 128)
    profile_rows = profile.reshape(pieces * 2 * slot * half, 128)
    d_rows = d_in.reshape(pieces * 2 * slot * half, 128)
    chunk, batch = 8, 4
    places = [(row, piece) for row in range(batch) for piece in range(pieces)]

    def d_copy(at):
        span = pl.ds(pl.multiple_of(at * chunk, chunk), chunk)
        return pltpu.make_async_remote_copy(
            src_ref=d_in.at[:, pl.ds(far_slot, levels), span, :],
            dst_ref=d_far.at[:, :, span, :],
            send_sem=d_sems.at[0, at], recv_sem=d_sems.at[1, at],
            device_id={"lev": other}, device_id_type=MESH,
        )

    def out_copy(at, side):
        first = own_row if side == 0 else far_row
        span = pl.ds(pl.multiple_of(first + at * chunk, chunk), chunk)
        return pltpu.make_async_copy(
            zonal.at[:, span, :], out_hbm.at[:, span, :], out_sems.at[side, at]
        )

    nt = (((1,), (1,)), ((), ()))

    def network(at, carry):
        for sub in range(chunk // batch):
            first = at * chunk + sub * batch
            x_parts, b_parts = [], []
            for row, piece in places:
                r = first + row
                x_parts.append(
                    profile_rows[pl.ds(piece * 2 * slot * half + r, 2 * slot, stride=half), :].astype(jnp.bfloat16)
                )
                own = v_rows[pl.ds(piece * slot * rows + own_row + r, slot, stride=rows), :]
                far = far_rows[pl.ds(piece * slot * half + r, slot, stride=half), :]
                low_half = jnp.where(lev == 0, own, far)
                high_half = jnp.where(lev == 0, far, own)
                b_parts.append(
                    jnp.concatenate([low_half, high_half], axis=0).astype(jnp.bfloat16)
                )
            flat = jnp.concatenate(x_parts, axis=1)
            back = jnp.concatenate(b_parts, axis=1)
            act = jnp.tanh(jnp.dot(w_in[...], flat, preferred_element_type=jnp.float32))
            d_act = jnp.dot(w_out[...], back, preferred_element_type=jnp.float32)
            d_pre = (d_act * (1.0 - act * act)).astype(jnp.bfloat16)
            of_out = lax.dot_general(
                act.astype(jnp.bfloat16), back, nt, preferred_element_type=jnp.float32
            )
            of_in = lax.dot_general(d_pre, flat, nt, preferred_element_type=jnp.float32)
            grad_ref[...] += jnp.concatenate([of_out, of_in], axis=1)
            d_input = jnp.dot(w_in_t[...], d_pre, preferred_element_type=jnp.float32)
            d_input = d_input.astype(jnp.bfloat16).astype(jnp.float32)
            for at_place, (row, piece) in enumerate(places):
                start = piece * 2 * slot * half + first + row
                d_rows[pl.ds(start, 2 * slot, stride=half), :] = (
                    d_input[:, at_place * 128 : at_place * 128 + 128]
                )
        d_copy(at).start()
        span = pl.ds(pl.multiple_of(at * chunk, chunk), chunk)
        own_span = pl.ds(pl.multiple_of(own_row + at * chunk, chunk), chunk)

        def body(z, carry):
            zonal[z, own_span, :] = whole(v, z, own_span) + whole(d_in, own_slot + z, span)
            return carry

        lax.fori_loop(0, levels, body, 0, unroll=5 if levels % 5 == 0 else 1)
        out_copy(at, 0).start()
        return carry

    chunks = half // chunk
    lax.fori_loop(0, chunks, network, 0)
    slotted = grad_ref[...]
    at_slot = lax.rem(lax.broadcasted_iota(jnp.int32, slotted.shape, 1), 2 * slot)
    grad_ref[...] = jnp.where(
        at_slot < levels, slotted,
        pltpu.roll(slotted, slotted.shape[1] - (slot - levels), axis=1),
    )

    def finish(at, carry):
        d_copy(at).wait_recv()
        span = pl.ds(pl.multiple_of(at * chunk, chunk), chunk)
        far_span = pl.ds(pl.multiple_of(far_row + at * chunk, chunk), chunk)

        def body(z, carry):
            zonal[z, far_span, :] = whole(v, z, far_span) + whole(d_far, z, span)
            return carry

        lax.fori_loop(0, levels, body, 0, unroll=5 if levels % 5 == 0 else 1)
        out_copy(at, 1).start()
        return carry

    lax.fori_loop(0, chunks, finish, 0)

    def drain(at, carry):
        d_copy(at).wait_send()
        out_copy(at, 0).wait()
        out_copy(at, 1).wait()
        return carry

    lax.fori_loop(0, chunks, drain, 0)
    theta_out.wait_send()
    for part in range(2):
        back_copy(part).wait_send()
    for step in range(STEPS):
        for part in range(2):
            x_copy(step, part).wait_send()

            @pl.when(sec > 0)
            def _():
                y_copy(step, part).wait_send()

        @pl.when(lev == 1)
        def _():
            z_copy(step).wait_send()


def columns_back(sizes, theta, seed, zonal, merid, updraft, weight_in, weight_out):
    levels, rows, lanes = seed.shape
    hidden, width = weight_out.shape[1], 4 * slot_size(levels)
    slot, half, pieces = width // 4, rows // 2, lanes // 128
    f32, bf16 = jnp.float32, jnp.bfloat16
    hbm = pl.BlockSpec(memory_space=pl.ANY)
    vmem = pl.BlockSpec(memory_space=pltpu.VMEM)
    dma = pltpu.SemaphoreType.DMA
    ratio = pltpu.VMEM((levels, rows, lanes), f32)
    return pl.pallas_call(
        functools.partial(column_kernel, sizes),
        out_shape=[
            jax.ShapeDtypeStruct((levels, rows, lanes), f32),
            jax.ShapeDtypeStruct((hidden, width), f32),
        ],
        in_specs=[pl.BlockSpec(memory_space=pltpu.HBM)] * 5 + [vmem] * 2,
        out_specs=[hbm, vmem],
        scratch_shapes=[
            pltpu.VMEM((pieces, slot, rows, 128), f32), ratio, ratio, ratio,
            pltpu.VMEM((STEPS, slot, lanes), f32), pltpu.VMEM((STEPS, slot, lanes), f32),
            pltpu.VMEM((STEPS, 2, 8, 128), f32), pltpu.VMEM((STEPS, 2, 8, 128), f32),
            pltpu.VMEM((STEPS, rows, lanes), f32), pltpu.VMEM((STEPS, rows, lanes), f32),
            pltpu.VMEM((levels, half, lanes), bf16), pltpu.VMEM((levels, half, lanes), bf16),
            pltpu.VMEM((pieces, 2 * slot, half, 128), f32),
            pltpu.VMEM((pieces, slot, half, 128), f32),
            pltpu.VMEM((pieces, 2 * slot, half, 128), f32),
            pltpu.VMEM((pieces, levels, half, 128), f32),
            pltpu.VMEM((hidden, width // 2), bf16), pltpu.VMEM((hidden, width // 2), bf16),
            pltpu.VMEM((width // 2, hidden), bf16),
            pltpu.VMEM((hidden, width), f32), pltpu.VMEM((width // 2, hidden), f32),
            dma((3, 2)), dma((pieces, 2)), dma((3,)), dma((2, STEPS, 2)), dma((2, STEPS, 2)), dma((2, STEPS)),
            dma((2, 2)), dma((2, half // 8)), dma((2, half // 8)),
        ],
        compiler_params=pltpu.CompilerParams(
            collective_id=2, has_side_effects=True, vmem_limit_bytes=48 * 1024 * 1024
        ),
        name="columns_back",
    )(theta, seed, zonal, merid, updraft, weight_in, weight_out)


def shards(
    thermal_departure,
    seed_sensitivity,
    zonal_flow_ratio,
    meridional_flow_ratio,
    updraft_flow_ratio,
    entry_layer_matrix,
    final_layer_matrix,
    mean_estimate_entry_matrix,
    squared_estimate_entry_matrix,
    mean_estimate_final_matrix,
    squared_estimate_final_matrix,
):
    total_cols = (
        seed_sensitivity.shape[1]
        * seed_sensitivity.shape[2]
        * lax.axis_size("col")
        * lax.axis_size("sec")
    )
    factor = 1.0 / math.sqrt(total_cols)
    sizes = tuple(lax.axis_size(axis) for axis in REDUCED)
    input_cotangent, grad = columns_back(
        sizes, thermal_departure, seed_sensitivity, zonal_flow_ratio, meridional_flow_ratio,
        updraft_flow_ratio, entry_layer_matrix, final_layer_matrix.T,
    )
    return input_cotangent, *reduce_update(
        sizes, factor, grad, entry_layer_matrix, final_layer_matrix,
        mean_estimate_entry_matrix, squared_estimate_entry_matrix,
        mean_estimate_final_matrix, squared_estimate_final_matrix,
    )


def solution(mesh):
    in_specs = (
        P("lev", ("group", "col"), "sec"),
        P("lev", ("group", "col"), "sec"),
        P("lev", ("group", "col"), "sec"),
        P("lev", ("group", "col"), "sec"),
        P("lev", ("group", "col"), "sec"),
        P(),
        P(),
        P(None, ("col", "sec", "lev")),
        P(None, ("col", "sec", "lev")),
        P(("col", "sec", "lev"), None),
        P(("col", "sec", "lev"), None),
    )
    out_specs = (
        P("lev", ("group", "col"), "sec"),
        P("group", None),
        P("group", None),
        P("group", ("col", "sec", "lev")),
        P("group", ("col", "sec", "lev")),
        P(("group", "col", "sec", "lev"), None),
        P(("group", "col", "sec", "lev"), None),
    )
    return jax.shard_map(shards, mesh=mesh, in_specs=in_specs, out_specs=out_specs, check_vma=False)
```
